32 devices in a mesh: op: 16 (over z, x, core), sec: 2 (over y).
Axes of the slice: x: 2, y: 2, z: 4, core: 2. Of those that a mesh axis runs over, the one named last changes fastest.
Arguments:
- psi: float32 [640, 2, 640], P('op', 'sec'), may hold values from -6 to 6
- left_env: float32 [16, 2, 640, 640], P('op', 'sec'), may hold values from -0.25 to 0.25
- right_env: float32 [16, 2, 640, 640], P('op', 'sec'), may hold values from -0.0625 to 0.0625
- denominators: float32 [640, 2, 640], P('op', 'sec'), may hold values from 0.5 to 4
- source_sector: int32 [16, 2], replicated, may hold values from 0 to 1
- owner: int32 [2], replicated, may hold values from 0 to 1, each once
- orders: int32 [2], replicated, may hold values from 480 to 640
Outputs:
- new_vector: float32 [640, 2, 640], P('op', 'sec')
- correction: float32 [640, 2, 640], P('op', 'sec')
The draws below stay inside these ranges and needn't reach their ends.
Inputs may be any that keep to these rules, and one draw needn't show every extreme that they name: `source_sector`: entry (t, s) is the sector from which term t maps into sector s. `owner`: each sector's slot; every slot holds one sector. Only the first orders rows and columns of a sector's block count; the inputs may hold any values beyond them, and the mask removes those entries.
All inputs are finite; a program needn't handle non-finite values.
Results may differ from the reference program's by a relative error of at most 0.0003.
Values sent between devices are 32-bit elements; how exact they have to be, the bound alone decides.
A program may use at most 64 MiB of HBM per device.

```python
import math
import jax
import jax.numpy as jnp
from jax import lax

MAXO = 640
NSEC = 2
TERMS = 16


def set_ends(result, stream_key, least, largest):
    shape = result.shape
    place = [jax.random.randint(jax.random.fold_in(stream_key, axis), (), 0, shape[axis]) for axis in range(len(shape))]
    result = result.at[tuple(place)].set(least)
    longest = shape.index(max(shape))
    place[longest] = (place[longest] + 1) % shape[longest]
    return result.at[tuple(place)].set(largest)


def levels(key, extent, cuts, least, largest):
    gain = 1.0
    for position, blocks in cuts:
        draws = jax.random.uniform(jax.random.fold_in(jax.random.fold_in(key, 6), position), (blocks,), jnp.float32, least / len(cuts), largest / len(cuts))
        gain = gain * jnp.repeat(jnp.exp(draws), extent[position] // blocks).reshape((-1,) + (1,) * (len(extent) - 1 - position))
    return gain


def bell_draw(own_key, extent, deviation, reach, cuts=(), held_as=jnp.bfloat16):
    values = deviation * jax.random.normal(own_key, extent, jnp.float32)
    if cuts:
        values = values * levels(own_key, extent, cuts, -0.22, 0.18)
    return jnp.clip(values, -reach, reach).astype(held_as)


def setup_inputs(seed: int = 0) -> dict:
    key_list = jax.random.split(jax.random.key(seed), 8)
    return {
        "psi": bell_draw(key_list[0], (MAXO, NSEC, MAXO), 1.0, 6.0, ((0, 16), (1, 2)), jnp.float32),
        "left_env": bell_draw(key_list[1], (TERMS, NSEC, MAXO, MAXO), MAXO ** -0.5, 0.25, ((0, 16), (1, 2)), jnp.float32),
        "right_env": bell_draw(key_list[2], (TERMS, NSEC, MAXO, MAXO), (MAXO * TERMS) ** -0.5, 0.0625, ((0, 16), (1, 2)), jnp.float32),
        "denominators": jnp.clip(jnp.exp(math.log(4.0) - 2.0794415 * jax.random.uniform(key_list[3], (MAXO, NSEC, MAXO), jnp.float32) ** levels(key_list[3], (MAXO, NSEC, MAXO), ((0, 16), (1, 2)), -0.2, 0.2)), 0.5, 4.0),
        "source_sector": set_ends(jax.random.randint(key_list[4], (TERMS, NSEC), 0, NSEC), jax.random.fold_in(key_list[4], 1), 0, NSEC - 1).astype(jnp.int32),
        "owner": jax.random.permutation(key_list[5], NSEC).astype(jnp.int32),
        "orders": jax.random.randint(key_list[6], (NSEC,), 3 * MAXO // 4, MAXO + 1).astype(jnp.int32),
    }


EPS = 1e-06
HIGH = lax.Precision.HIGHEST

def slot_sectors(owner):
    slots = jnp.arange(owner.shape[0], dtype=jnp.int32)
    hits = (owner[None, :] == slots[:, None]).astype(jnp.int32)
    return lax.optimization_barrier(jnp.sum(hits * slots[None, :], axis=1)).astype(jnp.int32)

def reference(psi, left_env, right_env, denominators, source_sector, owner, orders):
    sectors = slot_sectors(owner)
    order_slot = jnp.take(orders, sectors)
    line = jnp.arange(MAXO, dtype=jnp.int32)
    mask = ((line[:, None, None] < order_slot[None, :, None]) & (line[None, None, :] < order_slot[None, :, None])).astype(jnp.float32)
    source_slot = jnp.take(owner, jnp.take(source_sector, sectors, axis=1))
    count = float(MAXO * NSEC * MAXO)

    def apply(vector):

        def add_term(total, pieces):
            left, right, slots = pieces
            chosen = jnp.take(vector, slots, axis=1)
            inner = jnp.einsum('ajb,jbc->ajc', chosen, right, precision=HIGH)
            return (total + jnp.einsum('jxa,ajc->xjc', left, inner, precision=HIGH), None)
        total, _ = lax.scan(add_term, jnp.zeros_like(vector), (left_env, right_env, source_slot))
        return total * mask

    def inner_mean(first, second):
        return jnp.sum(first * second) / count
    v_raw = psi * mask
    w_raw = apply(v_raw)
    norm_raw = inner_mean(v_raw, v_raw)
    product_raw = inner_mean(v_raw, w_raw)
    scale = 1.0 / jnp.sqrt(norm_raw + EPS)
    v_zero = scale * v_raw
    w_zero = scale * w_raw
    rayleigh = product_raw / (norm_raw + EPS)
    update = (w_zero - rayleigh * v_zero) / denominators
    update_perp = update - inner_mean(v_zero, update) * v_zero
    v_one = update_perp / jnp.sqrt(inner_mean(update_perp, update_perp) + EPS)
    w_one = apply(v_one)
    corner = inner_mean(v_one, w_one)
    couple = inner_mean(v_one, w_zero)
    angle = 0.5 * jnp.arctan2(2.0 * couple, rayleigh - corner)
    sine = jnp.sin(angle)
    cosine = jnp.cos(angle)
    new_vector = sine * v_zero - cosine * v_one
    applied = sine * w_zero - cosine * w_one
    lam = sine * sine * rayleigh + cosine * cosine * corner - 2.0 * sine * cosine * couple
    correction = (applied - lam * new_vector) / denominators
    return (new_vector, correction)
```

```python
import functools

import jax
import jax.numpy as jnp
from jax import lax
from jax.experimental import pallas as pl
from jax.experimental.pallas import tpu as pltpu
from jax.sharding import PartitionSpec as P

EPS = 1e-06
HIGH = lax.Precision.HIGHEST
MESH = pl.DeviceIdType.MESH
F32 = jnp.float32
BF16 = jnp.bfloat16
ROWS = 8


def slot_sectors(owner):
    slots = jnp.arange(owner.shape[0], dtype=jnp.int32)
    hits = (owner[None, :] == slots[:, None]).astype(jnp.int32)
    return jnp.sum(hits * slots[None, :], axis=1)


def general(psi, left_env, right_env, denominators, source_sector, owner, orders):
    rows_here = psi.shape[0]
    sec_here = psi.shape[1]
    width = psi.shape[2]
    term_here = left_env.shape[0]
    op_size = lax.axis_size("op")
    sec_size = lax.axis_size("sec")
    op_pos = lax.axis_index("op")
    sec_pos = lax.axis_index("sec")
    sectors = slot_sectors(owner)
    sectors_here = lax.dynamic_slice_in_dim(sectors, sec_pos * sec_here, sec_here, 0)
    order_here = jnp.take(orders, sectors_here)
    row_ids = op_pos * rows_here + jnp.arange(rows_here, dtype=jnp.int32)
    col_ids = jnp.arange(width, dtype=jnp.int32)
    mask = (
        (row_ids[:, None, None] < order_here[None, :, None])
        & (col_ids[None, None, :] < order_here[None, :, None])
    ).astype(jnp.float32)
    source_all = jnp.take(owner, jnp.take(source_sector, sectors_here, axis=1))
    blocks = term_here * sec_here
    left_flat = left_env.reshape(blocks, width, width)
    right_flat = right_env.reshape(blocks, width, width)
    count = float(rows_here * sec_here * width * op_size * sec_size)

    def apply(vector):
        shard_all = lax.all_gather(vector, "sec", axis=1, tiled=True)
        outgoing = jnp.take(shard_all, source_all.reshape(-1), axis=1).reshape(
            rows_here, op_size, blocks, width
        )
        chosen = lax.all_to_all(outgoing, "op", split_axis=1, concat_axis=0, tiled=True).reshape(
            width, blocks, width
        )
        inner = jnp.einsum("apb,pbc->apc", chosen, right_flat, precision=HIGH)
        product = jnp.einsum("pxa,apc->xpc", left_flat, inner, precision=HIGH)
        whole = product.reshape(width, term_here, sec_here, width).sum(axis=1)
        summed = lax.psum_scatter(whole, "op", scatter_dimension=0, tiled=True)
        return summed * mask

    def partial_sum(first, second):
        return jnp.sum(first * second)

    v_raw = psi * mask
    w_raw = apply(v_raw)
    start_pair = lax.psum(
        jnp.stack([partial_sum(v_raw, v_raw), partial_sum(v_raw, w_raw)]), ("op", "sec")
    )
    norm_raw = start_pair[0] / count
    product_raw = start_pair[1] / count
    scale = 1.0 / jnp.sqrt(norm_raw + EPS)
    v_zero = scale * v_raw
    w_zero = scale * w_raw
    rayleigh = product_raw / (norm_raw + EPS)
    update = (w_zero - rayleigh * v_zero) / denominators
    along = lax.psum(partial_sum(v_zero, update), ("op", "sec")) / count
    update_perp = update - along * v_zero
    tail = lax.psum(partial_sum(update_perp, update_perp), ("op", "sec")) / count
    v_one = update_perp / jnp.sqrt(tail + EPS)
    w_one = apply(v_one)
    sub_pair = lax.psum(
        jnp.stack([partial_sum(v_one, w_one), partial_sum(v_one, w_zero)]), ("op", "sec")
    )
    corner = sub_pair[0] / count
    couple = sub_pair[1] / count
    angle = 0.5 * jnp.arctan2(2.0 * couple, rayleigh - corner)
    sine = jnp.sin(angle)
    cosine = jnp.cos(angle)
    new_vector = sine * v_zero - cosine * v_one
    applied = sine * w_zero - cosine * w_one
    lam = sine * sine * rayleigh + cosine * cosine * corner - 2.0 * sine * cosine * couple
    correction = (applied - lam * new_vector) / denominators
    return (new_vector, correction)


def split(value):
    high = value.astype(BF16)
    return high, (value - high.astype(F32)).astype(BF16)


def product3(ah, al, bh, bl):
    dot = functools.partial(jnp.dot, preferred_element_type=F32)
    return dot(ah, bh) + (dot(ah, bl) + dot(al, bh))


def kernel(
    dims, sec, psi_ref, left_hbm, right_hbm, den_ref, source_ref, owner_ref, orders_ref,
    new_ref, corr_ref, *scratch
):
    far, near, core = dims
    chunks = psi_ref.shape[0] // ROWS
    rows = psi_ref.shape[0]
    width = psi_ref.shape[1]
    op = far * near * core
    held = (scratch[:chunks], scratch[chunks : 2 * chunks])
    (left_f, right_f, left_h, left_l, right_h, right_l, inner, inner_h, inner_l, raw,
     applied, step, parts, got_core, got_near, got_far, tiles, got_tiles, load_sem,
     gather_send, gather_recv, sum_send, sum_recv, tile_send, tile_recv) = scratch[2 * chunks :]

    me = lax.axis_index("op")
    y = lax.axis_index("sec")
    c = lax.rem(me, core)
    b = lax.rem(lax.div(me, core), near)
    a = lax.div(me, core * near)
    where = {"far": a, "near": b, "core": c, "sec": y}
    size = {"far": far, "near": near, "core": core, "sec": sec}

    def turned(axis, by):
        place = dict(where)
        place[axis] = lax.rem(where[axis] + by + size[axis], size[axis])
        return place

    def device(place):
        return ((place["far"] * near + place["near"]) * core + place["core"], place["sec"])

    every = [(axis, d) for axis in ("far", "near", "sec", "core") for d in range(1, size[axis])]

    loads = [
        pltpu.make_async_copy(right_hbm, right_f, load_sem.at[0]),
        pltpu.make_async_copy(left_hbm, left_f, load_sem.at[1]),
    ]
    for load in loads:
        load.start()

    barrier = pltpu.get_barrier_semaphore()
    for axis, d in every:
        pl.semaphore_signal(
            barrier, inc=1, device_id=device(turned(axis, d)), device_id_type=MESH
        )

    sector = jnp.int32(0)
    for s in range(sec):
        sector = sector + jnp.where(owner_ref[s] == y, s, 0)
    order = orders_ref[sector]
    source = owner_ref[source_ref[me, sector]]

    row_ids = lax.broadcasted_iota(jnp.int32, (rows, width), 0) + me * rows
    col_ids = lax.broadcasted_iota(jnp.int32, (rows, width), 1)
    mask = ((row_ids < order) & (col_ids < order)).astype(F32)
    raw[...] = psi_ref[...] * mask
    for k in range(chunks):
        held[0][k][y, a, b, c] = raw[pl.ds(k * ROWS, ROWS), :]

    pl.semaphore_wait(barrier, len(every))

    def area(axes, place):
        pick = lambda axis: slice(None) if axis in axes else place[axis]
        return (pick("sec"), pick("far"), pick("near"), pick("core"))

    def sequence(k):
        return ("far", "near", "sec", "core") if k % 2 == 0 else ("far", "sec", "near", "core")

    slot_of = {pair: n for n, pair in enumerate(every)}

    def gather_copy(turn, k, stage, d, from_place, to_place):
        axes = sequence(k)
        block = held[turn][k].at[area(axes[:stage], from_place)]
        n = slot_of[(axes[stage], d)]
        return pltpu.make_async_remote_copy(
            src_ref=block, dst_ref=block,
            send_sem=gather_send.at[turn, k, n], recv_sem=gather_recv.at[turn, k, n],
            device_id=device(to_place), device_id_type=MESH,
        )

    def gather_start(turn, k, stage):
        axis = sequence(k)[stage]
        for d in range(1, size[axis]):
            gather_copy(turn, k, stage, d, where, turned(axis, d)).start()

    def gather_wait(turn, k, stage):
        axis = sequence(k)[stage]
        for d in range(1, size[axis]):
            gather_copy(turn, k, stage, d, turned(axis, -d), turned(axis, d)).wait_recv()

    def gather_end(turn):
        for k in range(chunks):
            for stage, axis in enumerate(sequence(k)):
                for d in range(1, size[axis]):
                    gather_copy(turn, k, stage, d, where, turned(axis, d)).wait_send()

    def tile_copy(red, stage, d):
        axis = ("far", "near", "sec", "core")[stage]
        n = slot_of[(axis, d)]
        return pltpu.make_async_remote_copy(
            src_ref=tiles.at[red, stage], dst_ref=got_tiles.at[red, n],
            send_sem=tile_send.at[red, n], recv_sem=tile_recv.at[red, n],
            device_id=device(turned(axis, d)), device_id_type=MESH,
        )

    def tile_start(red, stage, values=None):
        axis = ("far", "near", "sec", "core")[stage]
        if values is not None:
            line = lax.broadcasted_iota(jnp.int32, tiles.shape[2:], 0)
            tile = jnp.zeros(tiles.shape[2:], F32)
            for n, value in enumerate(values):
                tile = jnp.where(line == n, value, tile)
            tiles[red, stage] = tile
        for d in range(1, size[axis]):
            tile_copy(red, stage, d).start()

    def tile_wait(red, stage):
        axis = ("far", "near", "sec", "core")[stage]
        total = tiles[red, stage]
        for d in range(1, size[axis]):
            tile_copy(red, stage, d).wait_recv()
            total = total + got_tiles[red, slot_of[(axis, d)]]
        tiles[red, stage + 1] = total

    def tile_advance(red, stage):
        tile_wait(red, stage)
        if stage < 3:
            tile_start(red, stage + 1)

    count = float(rows * width * op * sec)

    def tile_read(red, n):
        return tiles[red, 4, pl.ds(n, 1), pl.ds(0, 1)] / count

    def total(value):
        return jnp.sum(value.reshape(-1, width), keepdims=True)

    def core_copy(turn, k, d):
        place = turned("core", d)
        return pltpu.make_async_remote_copy(
            src_ref=parts.at[turn, k, :, :, place["core"]], dst_ref=got_core.at[turn, k, d - 1],
            send_sem=sum_send.at[turn, k, slot_of[("core", d)]],
            recv_sem=sum_recv.at[turn, k, slot_of[("core", d)]],
            device_id=device(place), device_id_type=MESH,
        )

    def near_copy(turn, k, d):
        place = turned("near", d)
        return pltpu.make_async_remote_copy(
            src_ref=parts.at[turn, k, :, place["near"], c], dst_ref=got_near.at[turn, k, d - 1],
            send_sem=sum_send.at[turn, k, slot_of[("near", d)]],
            recv_sem=sum_recv.at[turn, k, slot_of[("near", d)]],
            device_id=device(place), device_id_type=MESH,
        )

    def far_copy(turn, k, d):
        place = turned("far", d)
        return pltpu.make_async_remote_copy(
            src_ref=parts.at[turn, k, place["far"], b, c], dst_ref=got_far.at[turn, k, d - 1],
            send_sem=sum_send.at[turn, k, slot_of[("far", d)]],
            recv_sem=sum_recv.at[turn, k, slot_of[("far", d)]],
            device_id=device(place), device_id_type=MESH,
        )

    def sum_core(turn, k):
        for d in range(1, core):
            core_copy(turn, k, d).wait_recv()
        mine = parts[turn, k, :, :, c]
        for d in range(1, core):
            mine = mine + got_core[turn, k, d - 1]
        parts[turn, k, :, :, c] = mine
        for d in range(1, near):
            near_copy(turn, k, d).start()

    def sum_near(turn, k):
        for d in range(1, near):
            near_copy(turn, k, d).wait_recv()
        mine = parts[turn, k, :, b, c]
        for d in range(1, near):
            mine = mine + got_near[turn, k, d - 1]
        parts[turn, k, :, b, c] = mine
        for d in range(1, far):
            far_copy(turn, k, d).start()

    def sum_far(turn, k):
        for d in range(1, far):
            far_copy(turn, k, d).wait_recv()
        mine = parts[turn, k, a, b, c]
        for d in range(1, far):
            mine = mine + got_far[turn, k, d - 1]
        return mine

    def sum_end(turn):
        for k in range(chunks):
            for n in range(1, core):
                core_copy(turn, k, n).wait_send()
            for n in range(1, near):
                near_copy(turn, k, n).wait_send()
            for n in range(1, far):
                far_copy(turn, k, n).wait_send()

    def matmuls(turn):
        for k in range(chunks):
            gather_wait(turn, k, 3)
            high, low = split(held[turn][k][source].reshape(op * ROWS, width))
            inner[:, pl.ds(k * ROWS, ROWS), :] = product3(
                high, low, right_h[...], right_l[...]
            ).reshape(op, ROWS, width)
        whole = inner[...].reshape(op * rows, width)
        high, low = split(whole)
        inner_h[...] = high
        inner_l[...] = low

        @pl.loop(0, chunks)
        def _(k):
            out = product3(left_h[k], left_l[k], inner_h[...], inner_l[...])
            parts[turn, k] = out.reshape(far, near, core, ROWS, width)
            for d in range(1, core):
                core_copy(turn, k, d).start()

    for k in range(chunks):
        gather_start(0, k, 0)
    loads[0].wait()
    high, low = split(right_f[...])
    right_h[...] = high
    right_l[...] = low
    norm_part = total(raw[...] * raw[...])
    for k in range(chunks):
        gather_wait(0, k, 0)
        gather_start(0, k, 1)
    loads[1].wait()
    for k in range(chunks):
        high, low = split(left_f[:, pl.ds(k * ROWS, ROWS), :].reshape(op * ROWS, width))
        left_h[k] = high
        left_l[k] = low
    for stage in (1, 2):
        for k in range(chunks):
            gather_wait(0, k, stage)
            gather_start(0, k, stage + 1)
    matmuls(0)
    along_part = jnp.zeros((1, 1), F32)
    for k in range(chunks):
        along_part = along_part + total(held[0][k][y] * parts[0, k])
        sum_core(0, k)
    tile_start(0, 0, (norm_part, along_part))
    for k in range(chunks):
        sum_near(0, k)
        if k < 4:
            tile_advance(0, k)
    for k in range(min(chunks, 4), 4):
        tile_advance(0, k)

    norm_raw = tile_read(0, 0)
    product_raw = tile_read(0, 1)
    scale = 1.0 / jnp.sqrt(norm_raw + EPS)
    rayleigh = product_raw / (norm_raw + EPS)
    along_part = jnp.zeros((1, 1), F32)
    for k in range(chunks):
        here = pl.ds(k * ROWS, ROWS)
        v_zero = scale * raw[here, :]
        w_zero = scale * (sum_far(0, k) * mask[k * ROWS : (k + 1) * ROWS])
        update = (w_zero - rayleigh * v_zero) / den_ref[here, :]
        applied[here, :] = w_zero
        step[here, :] = update
        held[1][k][y, a, b, c] = update
        gather_start(1, k, 0)
        along_part = along_part + total(v_zero * update)

    tile_start(1, 0, (along_part,))
    for stage in range(3):
        for k in range(chunks):
            gather_wait(1, k, stage)
            gather_start(1, k, stage + 1)
        tile_advance(1, stage)
    tile_advance(1, 3)
    along = tile_read(1, 0)
    v_zero = scale * raw[...]
    update_perp = step[...] - along * v_zero
    step[...] = update_perp
    tail_part = total(update_perp * update_perp)
    couple_part = total(update_perp * applied[...])
    matmuls(1)
    corner_part = jnp.zeros((1, 1), F32)
    shift = along * scale
    for k in range(chunks):
        corner_part = corner_part + total((held[1][k][y] - shift * held[0][k][y]) * parts[1, k])
        sum_core(1, k)
    tile_start(2, 0, (tail_part, couple_part, corner_part))
    for k in range(chunks):
        sum_near(1, k)
        if k < 4:
            tile_advance(2, k)
    for k in range(min(chunks, 4), 4):
        tile_advance(2, k)

    tail = tile_read(2, 0)
    perp_w_zero = tile_read(2, 1)
    perp_w = tile_read(2, 2) - along * perp_w_zero
    gain = 1.0 / jnp.sqrt(tail + EPS)
    corner = gain * gain * perp_w
    couple = gain * perp_w_zero
    down, across = 2.0 * couple, rayleigh - corner
    most = jnp.maximum(jnp.abs(down), jnp.abs(across))
    safe = jnp.where(most > 0.0, most, 1.0)
    down, across = down / safe, jnp.where(most > 0.0, across / safe, 1.0)
    length = jnp.sqrt(down * down + across * across)
    larger = jnp.sqrt(0.5 * (1.0 + jnp.abs(across) / length))
    smaller = 0.5 * jnp.abs(down) / (length * larger)
    sign = jnp.where(down < 0.0, -1.0, 1.0)
    cosine = jnp.where(across >= 0.0, larger, smaller)
    sine = sign * jnp.where(across >= 0.0, smaller, larger)
    lam = sine * sine * rayleigh + cosine * cosine * corner - 2.0 * sine * cosine * couple
    for k in range(chunks):
        here = pl.ds(k * ROWS, ROWS)
        w_zero = applied[here, :]
        w_one = gain * (sum_far(1, k) * mask[k * ROWS : (k + 1) * ROWS] - along * w_zero)
        new_vector = sine * (scale * raw[here, :]) - cosine * (gain * step[here, :])
        mixed = sine * w_zero - cosine * w_one
        new_ref[here, :] = new_vector
        corr_ref[here, :] = (mixed - lam * new_vector) / den_ref[here, :]

    for turn in range(2):
        gather_end(turn)
        sum_end(turn)
    for red in range(3):
        for stage, axis in enumerate(("far", "near", "sec", "core")):
            for d in range(1, size[axis]):
                tile_copy(red, stage, d).wait_send()


def fused(dims, sec, psi, left_env, right_env, denominators, source_sector, owner, orders):
    rows, _, width = psi.shape
    far, near, core = dims
    op = far * near * core
    chunks = rows // ROWS
    peers = far + near + core + sec - 4
    vmem = pl.BlockSpec(memory_space=pltpu.VMEM)
    smem = pl.BlockSpec(memory_space=pltpu.SMEM)
    hbm = pl.BlockSpec(memory_space=pl.ANY)
    block = (ROWS, width)
    scratch = [pltpu.VMEM((sec, far, near, core) + block, F32)] * (2 * chunks) + [
        pltpu.VMEM((op, rows, width), F32),
        pltpu.VMEM((width, width), F32),
        pltpu.VMEM((chunks, op * ROWS, width), BF16),
        pltpu.VMEM((chunks, op * ROWS, width), BF16),
        pltpu.VMEM((width, width), BF16),
        pltpu.VMEM((width, width), BF16),
        pltpu.VMEM((op, rows, width), F32),
        pltpu.VMEM((op * rows, width), BF16),
        pltpu.VMEM((op * rows, width), BF16),
        pltpu.VMEM((rows, width), F32),
        pltpu.VMEM((rows, width), F32),
        pltpu.VMEM((rows, width), F32),
        pltpu.VMEM((2, chunks, far, near, core) + block, F32),
        pltpu.VMEM((2, chunks, core - 1, far, near) + block, F32),
        pltpu.VMEM((2, chunks, near - 1, far) + block, F32),
        pltpu.VMEM((2, chunks, far - 1) + block, F32),
        pltpu.VMEM((3, 5, 8, 128), F32),
        pltpu.VMEM((3, peers, 8, 128), F32),
        pltpu.SemaphoreType.DMA((2,)),
        pltpu.SemaphoreType.DMA((2, chunks, peers)),
        pltpu.SemaphoreType.DMA((2, chunks, peers)),
        pltpu.SemaphoreType.DMA((2, chunks, peers)),
        pltpu.SemaphoreType.DMA((2, chunks, peers)),
        pltpu.SemaphoreType.DMA((3, peers)),
        pltpu.SemaphoreType.DMA((3, peers)),
    ]
    flat = jax.ShapeDtypeStruct((rows, width), F32)
    new_vector, correction = pl.pallas_call(
        functools.partial(kernel, dims, sec),
        out_shape=(flat, flat),
        in_specs=[vmem, hbm, hbm, vmem, smem, smem, smem],
        out_specs=(vmem, vmem),
        scratch_shapes=scratch,
        compiler_params=pltpu.CompilerParams(
            collective_id=0, has_side_effects=True, vmem_limit_bytes=52 * 2**20
        ),
    )(
        psi.reshape(rows, width),
        left_env.reshape(op, rows, width),
        right_env.reshape(width, width),
        denominators.reshape(rows, width),
        source_sector,
        owner,
        orders,
    )
    return new_vector.reshape(psi.shape), correction.reshape(psi.shape)


def per_device(*arrays):
    psi, left_env = arrays[0], arrays[1]
    op = lax.axis_size("op")
    sec = lax.axis_size("sec")
    rows, sec_here, width = psi.shape
    core = 2 if op % 2 == 0 else 1
    chips = op // core
    near = max(n for n in range(1, chips + 1) if chips % n == 0 and n * n <= chips)
    dims = (chips // near, near, core)
    fits = rows % ROWS == 0 and width % 128 == 0 and left_env.shape[:2] == (1, 1)
    if fits and sec_here == 1 and min(dims) > 1 and sec > 1 and op * rows == width:
        return fused(dims, sec, *arrays)
    return general(*arrays)


def solution(mesh):
    placed = (
        P("op", "sec", None),
        P("op", "sec", None, None),
        P("op", "sec", None, None),
        P("op", "sec", None),
        P(),
        P(),
        P(),
    )
    return jax.shard_map(
        per_device,
        mesh=mesh,
        in_specs=placed,
        out_specs=(P("op", "sec", None), P("op", "sec", None)),
        check_vma=False,
    )
```

```python
import functools

import jax
import jax.numpy as jnp
from jax import lax
from jax.experimental import pallas as pl
from jax.experimental.pallas import tpu as pltpu
from jax.sharding import PartitionSpec as P

EPS = 1e-06
HIGH = lax.Precision.HIGHEST
MESH = pl.DeviceIdType.MESH
F32 = jnp.float32
BF16 = jnp.bfloat16
ROWS = 8


def slot_sectors(owner):
    slots = jnp.arange(owner.shape[0], dtype=jnp.int32)
    hits = (owner[None, :] == slots[:, None]).astype(jnp.int32)
    return jnp.sum(hits * slots[None, :], axis=1)


def general(psi, left_env, right_env, denominators, source_sector, owner, orders):
    rows_here = psi.shape[0]
    sec_here = psi.shape[1]
    width = psi.shape[2]
    term_here = left_env.shape[0]
    op_size = lax.axis_size("op")
    sec_size = lax.axis_size("sec")
    op_pos = lax.axis_index("op")
    sec_pos = lax.axis_index("sec")
    sectors = slot_sectors(owner)
    sectors_here = lax.dynamic_slice_in_dim(sectors, sec_pos * sec_here, sec_here, 0)
    order_here = jnp.take(orders, sectors_here)
    row_ids = op_pos * rows_here + jnp.arange(rows_here, dtype=jnp.int32)
    col_ids = jnp.arange(width, dtype=jnp.int32)
    mask = (
        (row_ids[:, None, None] < order_here[None, :, None])
        & (col_ids[None, None, :] < order_here[None, :, None])
    ).astype(jnp.float32)
    source_all = jnp.take(owner, jnp.take(source_sector, sectors_here, axis=1))
    blocks = term_here * sec_here
    left_flat = left_env.reshape(blocks, width, width)
    right_flat = right_env.reshape(blocks, width, width)
    count = float(rows_here * sec_here * width * op_size * sec_size)

    def apply(vector):
        shard_all = lax.all_gather(vector, "sec", axis=1, tiled=True)
        outgoing = jnp.take(shard_all, source_all.reshape(-1), axis=1).reshape(
            rows_here, op_size, blocks, width
        )
        chosen = lax.all_to_all(outgoing, "op", split_axis=1, concat_axis=0, tiled=True).reshape(
            width, blocks, width
        )
        inner = jnp.einsum("apb,pbc->apc", chosen, right_flat, precision=HIGH)
        product = jnp.einsum("pxa,apc->xpc", left_flat, inner, precision=HIGH)
        whole = product.reshape(width, term_here, sec_here, width).sum(axis=1)
        summed = lax.psum_scatter(whole, "op", scatter_dimension=0, tiled=True)
        return summed * mask

    def partial_sum(first, second):
        return jnp.sum(first * second)

    v_raw = psi * mask
    w_raw = apply(v_raw)
    start_pair = lax.psum(
        jnp.stack([partial_sum(v_raw, v_raw), partial_sum(v_raw, w_raw)]), ("op", "sec")
    )
    norm_raw = start_pair[0] / count
    product_raw = start_pair[1] / count
    scale = 1.0 / jnp.sqrt(norm_raw + EPS)
    v_zero = scale * v_raw
    w_zero = scale * w_raw
    rayleigh = product_raw / (norm_raw + EPS)
    update = (w_zero - rayleigh * v_zero) / denominators
    along = lax.psum(partial_sum(v_zero, update), ("op", "sec")) / count
    update_perp = update - along * v_zero
    tail = lax.psum(partial_sum(update_perp, update_perp), ("op", "sec")) / count
    v_one = update_perp / jnp.sqrt(tail + EPS)
    w_one = apply(v_one)
    sub_pair = lax.psum(
        jnp.stack([partial_sum(v_one, w_one), partial_sum(v_one, w_zero)]), ("op", "sec")
    )
    corner = sub_pair[0] / count
    couple = sub_pair[1] / count
    angle = 0.5 * jnp.arctan2(2.0 * couple, rayleigh - corner)
    sine = jnp.sin(angle)
    cosine = jnp.cos(angle)
    new_vector = sine * v_zero - cosine * v_one
    applied = sine * w_zero - cosine * w_one
    lam = sine * sine * rayleigh + cosine * cosine * corner - 2.0 * sine * cosine * couple
    correction = (applied - lam * new_vector) / denominators
    return (new_vector, correction)


def split(value):
    high = value.astype(BF16)
    return high, (value - high.astype(F32)).astype(BF16)


def product3(ah, al, bh, bl):
    dot = functools.partial(jnp.dot, preferred_element_type=F32)
    return dot(ah, bh) + (dot(ah, bl) + dot(al, bh))


def end_scalars(tile_read, along, rayleigh):
    tail = tile_read(2, 0)
    perp_w_zero = tile_read(2, 1)
    perp_w = tile_read(2, 2) - along * perp_w_zero
    gain = 1.0 / jnp.sqrt(tail + EPS)
    corner = gain * gain * perp_w
    couple = gain * perp_w_zero
    down, across = 2.0 * couple, rayleigh - corner
    most = jnp.maximum(jnp.abs(down), jnp.abs(across))
    safe = jnp.where(most > 0.0, most, 1.0)
    down, across = down / safe, jnp.where(most > 0.0, across / safe, 1.0)
    length = jnp.sqrt(down * down + across * across)
    larger = jnp.sqrt(0.5 * (1.0 + jnp.abs(across) / length))
    smaller = 0.5 * jnp.abs(down) / (length * larger)
    sign = jnp.where(down < 0.0, -1.0, 1.0)
    cosine = jnp.where(across >= 0.0, larger, smaller)
    sine = sign * jnp.where(across >= 0.0, smaller, larger)
    lam = sine * sine * rayleigh + cosine * cosine * corner - 2.0 * sine * cosine * couple
    return gain, sine, cosine, lam


def kernel(
    dims, sec, psi_ref, left_hbm, right_hbm, den_ref, source_ref, owner_ref, orders_ref,
    new_ref, corr_ref, *scratch
):
    far, near, core = dims
    chunks = psi_ref.shape[0] // ROWS
    rows = psi_ref.shape[0]
    width = psi_ref.shape[1]
    op = far * near * core
    held = (scratch[:chunks], scratch[chunks : 2 * chunks])
    (left_f, right_f, left_h, left_l, right_h, right_l, inner, inner_h, inner_l, raw,
     applied, step, parts, got_core, got_near, got_far, tiles, got_tiles, load_sem,
     gather_send, gather_recv, sum_send, sum_recv, tile_send, tile_recv) = scratch[2 * chunks :]

    me = lax.axis_index("op")
    y = lax.axis_index("sec")
    c = lax.rem(me, core)
    b = lax.rem(lax.div(me, core), near)
    a = lax.div(me, core * near)
    where = {"far": a, "near": b, "core": c, "sec": y}
    size = {"far": far, "near": near, "core": core, "sec": sec}

    def turned(axis, by):
        place = dict(where)
        place[axis] = lax.rem(where[axis] + by + size[axis], size[axis])
        return place

    def device(place):
        return ((place["far"] * near + place["near"]) * core + place["core"], place["sec"])

    every = [(axis, d) for axis in ("far", "near", "sec", "core") for d in range(1, size[axis])]
    around = [
        (("near", i), ("core", j), ("sec", l))
        for i in range(near) for j in range(core) for l in range(sec) if i + j + l > 0
    ]
    along_far = [(("far", d),) for d in range(1, far)]

    def moved(offset):
        place = dict(where)
        for axis, by in offset:
            place[axis] = lax.rem(where[axis] + by, size[axis])
        return place

    loads = [
        pltpu.make_async_copy(right_hbm, right_f, load_sem.at[0]),
        pltpu.make_async_copy(left_hbm, left_f, load_sem.at[1]),
    ]
    for load in loads:
        load.start()

    barrier = pltpu.get_barrier_semaphore()
    for offset in around + along_far:
        pl.semaphore_signal(
            barrier, inc=1, device_id=device(moved(offset)), device_id_type=MESH
        )

    sector = jnp.int32(0)
    for s in range(sec):
        sector = sector + jnp.where(owner_ref[s] == y, s, 0)
    order = orders_ref[sector]
    source = owner_ref[source_ref[me, sector]]

    row_ids = lax.broadcasted_iota(jnp.int32, (rows, width), 0) + me * rows
    col_ids = lax.broadcasted_iota(jnp.int32, (rows, width), 1)
    mask = ((row_ids < order) & (col_ids < order)).astype(F32)
    raw[...] = psi_ref[...] * mask
    for k in range(chunks):
        held[0][k][y, a, b, c] = raw[pl.ds(k * ROWS, ROWS), :]

    pl.semaphore_wait(barrier, len(around + along_far))

    def area(axes, place):
        pick = lambda axis: slice(None) if axis in axes else place[axis]
        return (pick("sec"), pick("far"), pick("near"), pick("core"))

    def sequence(k):
        return ("far", "near", "sec", "core") if k % 2 == 0 else ("far", "sec", "near", "core")

    slot_of = {pair: n for n, pair in enumerate(every)}

    def gather_copy(turn, k, stage, d, from_place, to_place):
        axes = sequence(k)
        block = held[turn][k].at[area(axes[:stage], from_place)]
        n = slot_of[(axes[stage], d)]
        return pltpu.make_async_remote_copy(
            src_ref=block, dst_ref=block,
            send_sem=gather_send.at[turn, k, n], recv_sem=gather_recv.at[turn, k, n],
            device_id=device(to_place), device_id_type=MESH,
        )

    def gather_start(turn, k, stage):
        axis = sequence(k)[stage]
        for d in range(1, size[axis]):
            gather_copy(turn, k, stage, d, where, turned(axis, d)).start()

    def gather_wait(turn, k, stage):
        axis = sequence(k)[stage]
        for d in range(1, size[axis]):
            gather_copy(turn, k, stage, d, turned(axis, -d), turned(axis, d)).wait_recv()

    def gather_end(turn):
        for k in range(chunks):
            for stage, axis in enumerate(sequence(k)):
                for d in range(1, size[axis]):
                    gather_copy(turn, k, stage, d, where, turned(axis, d)).wait_send()

    groups = (around, along_far)

    def tile_copy(red, stage, n):
        slot = n + stage * len(around)
        return pltpu.make_async_remote_copy(
            src_ref=tiles.at[red, stage], dst_ref=got_tiles.at[red, slot],
            send_sem=tile_send.at[red, slot], recv_sem=tile_recv.at[red, slot],
            device_id=device(moved(groups[stage][n])), device_id_type=MESH,
        )

    def tile_send_all(red, stage):
        for n in range(len(groups[stage])):
            tile_copy(red, stage, n).start()

    def tile_start(red, values):
        line = lax.broadcasted_iota(jnp.int32, (8, 128), 0)
        tile = jnp.zeros((8, 128), F32)
        for n, value in enumerate(values):
            tile = jnp.where(line == n, value, tile)
        tiles[red, 0] = tile
        tile_send_all(red, 0)

    def tile_advance(red, stage):
        total = tiles[red, stage]
        for n in range(len(groups[stage])):
            tile_copy(red, stage, n).wait_recv()
            total = total + got_tiles[red, n + stage * len(around)]
        tiles[red, stage + 1] = total
        if stage == 0:
            tile_send_all(red, 1)

    count = float(rows * width * op * sec)

    def tile_read(red, n):
        return tiles[red, 2, pl.ds(n, 1), pl.ds(0, 1)] / count

    def total(value):
        return jnp.sum(value.reshape(-1, width), keepdims=True)

    def core_copy(turn, k, d):
        place = turned("core", d)
        return pltpu.make_async_remote_copy(
            src_ref=parts.at[turn, k, :, :, place["core"]], dst_ref=got_core.at[turn, k, d - 1],
            send_sem=sum_send.at[turn, k, slot_of[("core", d)]],
            recv_sem=sum_recv.at[turn, k, slot_of[("core", d)]],
            device_id=device(place), device_id_type=MESH,
        )

    def near_copy(turn, k, d):
        place = turned("near", d)
        return pltpu.make_async_remote_copy(
            src_ref=parts.at[turn, k, :, place["near"], c], dst_ref=got_near.at[turn, k, d - 1],
            send_sem=sum_send.at[turn, k, slot_of[("near", d)]],
            recv_sem=sum_recv.at[turn, k, slot_of[("near", d)]],
            device_id=device(place), device_id_type=MESH,
        )

    def far_copy(turn, k, d):
        place = turned("far", d)
        return pltpu.make_async_remote_copy(
            src_ref=parts.at[turn, k, place["far"], b, c], dst_ref=got_far.at[turn, k, d - 1],
            send_sem=sum_send.at[turn, k, slot_of[("far", d)]],
            recv_sem=sum_recv.at[turn, k, slot_of[("far", d)]],
            device_id=device(place), device_id_type=MESH,
        )

    def sum_core(turn, k):
        for d in range(1, core):
            core_copy(turn, k, d).wait_recv()
        mine = parts[turn, k, :, :, c]
        for d in range(1, core):
            mine = mine + got_core[turn, k, d - 1]
        parts[turn, k, :, :, c] = mine
        for d in range(1, near):
            near_copy(turn, k, d).start()

    def sum_near(turn, k):
        for d in range(1, near):
            near_copy(turn, k, d).wait_recv()
        mine = parts[turn, k, :, b, c]
        for d in range(1, near):
            mine = mine + got_near[turn, k, d - 1]
        parts[turn, k, :, b, c] = mine
        for d in range(1, far):
            far_copy(turn, k, d).start()

    def sum_far(turn, k):
        for d in range(1, far):
            far_copy(turn, k, d).wait_recv()
        mine = parts[turn, k, a, b, c]
        for d in range(1, far):
            mine = mine + got_far[turn, k, d - 1]
        return mine

    def sum_end(turn):
        for k in range(chunks):
            for n in range(1, core):
                core_copy(turn, k, n).wait_send()
            for n in range(1, near):
                near_copy(turn, k, n).wait_send()
            for n in range(1, far):
                far_copy(turn, k, n).wait_send()

    def gather_rest(turn, beside):
        for k in range(chunks + 1):
            if k < chunks:
                gather_wait(turn, k, 0)
                gather_start(turn, k, 1)
                beside(k)
            if k > 0:
                gather_wait(turn, k - 1, 1)
                gather_start(turn, k - 1, 2)

    def matmuls(turn, weigh):
        for k in range(chunks + 1):
            if k < chunks:
                gather_wait(turn, k, 2)
                gather_start(turn, k, 3)
            if k > 0:
                gather_wait(turn, k - 1, 3)
                high, low = split(held[turn][k - 1][source].reshape(op * ROWS, width))
                inner[:, pl.ds((k - 1) * ROWS, ROWS), :] = product3(
                    high, low, right_h[...], right_l[...]
                ).reshape(op, ROWS, width)
        whole = inner[...].reshape(op * rows, width)
        high, low = split(whole)
        inner_h[...] = high
        inner_l[...] = low
        weighed = jnp.zeros((1, 1), F32)
        for k in range(chunks):
            out = product3(left_h[k], left_l[k], inner_h[...], inner_l[...])
            parts[turn, k] = out.reshape(far, near, core, ROWS, width)
            for d in range(1, core):
                core_copy(turn, k, d).start()
            weighed = weighed + total(weigh(k) * parts[turn, k])
            if k > 0:
                sum_core(turn, k - 1)
        sum_core(turn, chunks - 1)
        return weighed

    def finish(turn, red, ready, use):
        values = None
        for k in range(chunks + 2):
            if k < chunks:
                sum_near(turn, k)
            if k < 2:
                tile_advance(red, k)
            else:
                if k == 2:
                    values = ready()
                use(k - 2, values)

    for k in range(chunks):
        gather_start(0, k, 0)
    loads[0].wait()
    high, low = split(right_f[...])
    right_h[...] = high
    right_l[...] = low
    norm_part = total(raw[...] * raw[...])
    loads[1].wait()

    def split_left(k):
        high, low = split(left_f[:, pl.ds(k * ROWS, ROWS), :].reshape(op * ROWS, width))
        left_h[k] = high
        left_l[k] = low

    gather_rest(0, split_left)
    start_part = matmuls(0, lambda k: held[0][k][y])
    tile_start(0, (norm_part, start_part))

    def start_values():
        norm_raw = tile_read(0, 0)
        product_raw = tile_read(0, 1)
        return 1.0 / jnp.sqrt(norm_raw + EPS), product_raw / (norm_raw + EPS)

    kept = {"along": jnp.zeros((1, 1), F32)}

    def take_step(k, values):
        scale, rayleigh = values
        kept["scale"], kept["rayleigh"] = values
        here = pl.ds(k * ROWS, ROWS)
        v_zero = scale * raw[here, :]
        w_zero = scale * (sum_far(0, k) * mask[k * ROWS : (k + 1) * ROWS])
        update = (w_zero - rayleigh * v_zero) / den_ref[here, :]
        applied[here, :] = w_zero
        step[here, :] = update
        held[1][k][y, a, b, c] = update
        gather_start(1, k, 0)
        kept["along"] = kept["along"] + total(v_zero * update)

    finish(0, 0, start_values, take_step)
    scale, rayleigh = kept["scale"], kept["rayleigh"]

    tile_start(1, (kept["along"],))

    def sum_along(k):
        if k in (1, 3):
            tile_advance(1, k // 2)

    gather_rest(1, sum_along)
    for stage in range(2):
        if 2 * stage + 1 >= chunks:
            tile_advance(1, stage)
    along = tile_read(1, 0)
    v_zero = scale * raw[...]
    update_perp = step[...] - along * v_zero
    step[...] = update_perp
    tail_part = total(update_perp * update_perp)
    couple_part = total(update_perp * applied[...])
    shift = along * scale
    corner_part = matmuls(1, lambda k: held[1][k][y] - shift * held[0][k][y])
    tile_start(2, (tail_part, couple_part, corner_part))

    def end_values():
        return end_scalars(tile_read, along, rayleigh)

    def give(k, values):
        gain, sine, cosine, lam = values
        here = pl.ds(k * ROWS, ROWS)
        w_zero = applied[here, :]
        w_one = gain * (sum_far(1, k) * mask[k * ROWS : (k + 1) * ROWS] - along * w_zero)
        new_vector = sine * (scale * raw[here, :]) - cosine * (gain * step[here, :])
        mixed = sine * w_zero - cosine * w_one
        new_ref[here, :] = new_vector
        corr_ref[here, :] = (mixed - lam * new_vector) / den_ref[here, :]

    finish(1, 2, end_values, give)

    for turn in range(2):
        gather_end(turn)
        sum_end(turn)
    for red in range(3):
        for stage in range(2):
            for n in range(len(groups[stage])):
                tile_copy(red, stage, n).wait_send()


def fused(dims, sec, psi, left_env, right_env, denominators, source_sector, owner, orders):
    rows, _, width = psi.shape
    far, near, core = dims
    op = far * near * core
    chunks = rows // ROWS
    peers = far + near + core + sec - 4
    pairs = near * core * sec - 1 + far - 1
    vmem = pl.BlockSpec(memory_space=pltpu.VMEM)
    smem = pl.BlockSpec(memory_space=pltpu.SMEM)
    hbm = pl.BlockSpec(memory_space=pl.ANY)
    block = (ROWS, width)
    scratch = [pltpu.VMEM((sec, far, near, core) + block, F32)] * (2 * chunks) + [
        pltpu.VMEM((op, rows, width), F32),
        pltpu.VMEM((width, width), F32),
        pltpu.VMEM((chunks, op * ROWS, width), BF16),
        pltpu.VMEM((chunks, op * ROWS, width), BF16),
        pltpu.VMEM((width, width), BF16),
        pltpu.VMEM((width, width), BF16),
        pltpu.VMEM((op, rows, width), F32),
        pltpu.VMEM((op * rows, width), BF16),
        pltpu.VMEM((op * rows, width), BF16),
        pltpu.VMEM((rows, width), F32),
        pltpu.VMEM((rows, width), F32),
        pltpu.VMEM((rows, width), F32),
        pltpu.VMEM((2, chunks, far, near, core) + block, F32),
        pltpu.VMEM((2, chunks, core - 1, far, near) + block, F32),
        pltpu.VMEM((2, chunks, near - 1, far) + block, F32),
        pltpu.VMEM((2, chunks, far - 1) + block, F32),
        pltpu.VMEM((3, 3, 8, 128), F32),
        pltpu.VMEM((3, pairs, 8, 128), F32),
        pltpu.SemaphoreType.DMA((2,)),
        pltpu.SemaphoreType.DMA((2, chunks, peers)),
        pltpu.SemaphoreType.DMA((2, chunks, peers)),
        pltpu.SemaphoreType.DMA((2, chunks, peers)),
        pltpu.SemaphoreType.DMA((2, chunks, peers)),
        pltpu.SemaphoreType.DMA((3, pairs)),
        pltpu.SemaphoreType.DMA((3, pairs)),
    ]
    flat = jax.ShapeDtypeStruct((rows, width), F32)
    new_vector, correction = pl.pallas_call(
        functools.partial(kernel, dims, sec),
        out_shape=(flat, flat),
        in_specs=[vmem, hbm, hbm, vmem, smem, smem, smem],
        out_specs=(vmem, vmem),
        scratch_shapes=scratch,
        compiler_params=pltpu.CompilerParams(
            collective_id=0, has_side_effects=True, vmem_limit_bytes=52 * 2**20
        ),
    )(
        psi.reshape(rows, width),
        left_env.reshape(op, rows, width),
        right_env.reshape(width, width),
        denominators.reshape(rows, width),
        source_sector,
        owner,
        orders,
    )
    return new_vector.reshape(psi.shape), correction.reshape(psi.shape)


def per_device(*arrays):
    psi, left_env = arrays[0], arrays[1]
    op = lax.axis_size("op")
    sec = lax.axis_size("sec")
    rows, sec_here, width = psi.shape
    core = 2 if op % 2 == 0 else 1
    chips = op // core
    near = max(n for n in range(1, chips + 1) if chips % n == 0 and n * n <= chips)
    dims = (chips // near, near, core)
    fits = rows % ROWS == 0 and width % 128 == 0 and left_env.shape[:2] == (1, 1)
    if fits and sec_here == 1 and min(dims) > 1 and sec > 1 and op * rows == width:
        return fused(dims, sec, *arrays)
    return general(*arrays)


def solution(mesh):
    placed = (
        P("op", "sec", None),
        P("op", "sec", None, None),
        P("op", "sec", None, None),
        P("op", "sec", None),
        P(),
        P(),
        P(),
    )
    return jax.shard_map(
        per_device,
        mesh=mesh,
        in_specs=placed,
        out_specs=(P("op", "sec", None), P("op", "sec", None)),
        check_vma=False,
    )
```

```python
import functools

import jax
import jax.numpy as jnp
from jax import lax
from jax.experimental import pallas as pl
from jax.experimental.pallas import tpu as pltpu
from jax.sharding import PartitionSpec as P

EPS = 1e-06
HIGH = lax.Precision.HIGHEST
MESH = pl.DeviceIdType.MESH
F32 = jnp.float32
BF16 = jnp.bfloat16
ROWS = 8


def slot_sectors(owner):
    slots = jnp.arange(owner.shape[0], dtype=jnp.int32)
    hits = (owner[None, :] == slots[:, None]).astype(jnp.int32)
    return jnp.sum(hits * slots[None, :], axis=1)


def general(psi, left_env, right_env, denominators, source_sector, owner, orders):
    rows_here = psi.shape[0]
    sec_here = psi.shape[1]
    width = psi.shape[2]
    term_here = left_env.shape[0]
    op_size = lax.axis_size("op")
    sec_size = lax.axis_size("sec")
    op_pos = lax.axis_index("op")
    sec_pos = lax.axis_index("sec")
    sectors = slot_sectors(owner)
    sectors_here = lax.dynamic_slice_in_dim(sectors, sec_pos * sec_here, sec_here, 0)
    order_here = jnp.take(orders, sectors_here)
    row_ids = op_pos * rows_here + jnp.arange(rows_here, dtype=jnp.int32)
    col_ids = jnp.arange(width, dtype=jnp.int32)
    mask = (
        (row_ids[:, None, None] < order_here[None, :, None])
        & (col_ids[None, None, :] < order_here[None, :, None])
    ).astype(jnp.float32)
    source_all = jnp.take(owner, jnp.take(source_sector, sectors_here, axis=1))
    blocks = term_here * sec_here
    left_flat = left_env.reshape(blocks, width, width)
    right_flat = right_env.reshape(blocks, width, width)
    count = float(rows_here * sec_here * width * op_size * sec_size)

    def apply(vector):
        shard_all = lax.all_gather(vector, "sec", axis=1, tiled=True)
        outgoing = jnp.take(shard_all, source_all.reshape(-1), axis=1).reshape(
            rows_here, op_size, blocks, width
        )
        chosen = lax.all_to_all(outgoing, "op", split_axis=1, concat_axis=0, tiled=True).reshape(
            width, blocks, width
        )
        inner = jnp.einsum("apb,pbc->apc", chosen, right_flat, precision=HIGH)
        product = jnp.einsum("pxa,apc->xpc", left_flat, inner, precision=HIGH)
        whole = product.reshape(width, term_here, sec_here, width).sum(axis=1)
        summed = lax.psum_scatter(whole, "op", scatter_dimension=0, tiled=True)
        return summed * mask

    def partial_sum(first, second):
        return jnp.sum(first * second)

    v_raw = psi * mask
    w_raw = apply(v_raw)
    start_pair = lax.psum(
        jnp.stack([partial_sum(v_raw, v_raw), partial_sum(v_raw, w_raw)]), ("op", "sec")
    )
    norm_raw = start_pair[0] / count
    product_raw = start_pair[1] / count
    scale = 1.0 / jnp.sqrt(norm_raw + EPS)
    v_zero = scale * v_raw
    w_zero = scale * w_raw
    rayleigh = product_raw / (norm_raw + EPS)
    update = (w_zero - rayleigh * v_zero) / denominators
    along = lax.psum(partial_sum(v_zero, update), ("op", "sec")) / count
    update_perp = update - along * v_zero
    tail = lax.psum(partial_sum(update_perp, update_perp), ("op", "sec")) / count
    v_one = update_perp / jnp.sqrt(tail + EPS)
    w_one = apply(v_one)
    sub_pair = lax.psum(
        jnp.stack([partial_sum(v_one, w_one), partial_sum(v_one, w_zero)]), ("op", "sec")
    )
    corner = sub_pair[0] / count
    couple = sub_pair[1] / count
    angle = 0.5 * jnp.arctan2(2.0 * couple, rayleigh - corner)
    sine = jnp.sin(angle)
    cosine = jnp.cos(angle)
    new_vector = sine * v_zero - cosine * v_one
    applied = sine * w_zero - cosine * w_one
    lam = sine * sine * rayleigh + cosine * cosine * corner - 2.0 * sine * cosine * couple
    correction = (applied - lam * new_vector) / denominators
    return (new_vector, correction)


def split(value):
    high = value.astype(BF16)
    return high, (value - high.astype(F32)).astype(BF16)


def product3(ah, al, bh, bl):
    dot = functools.partial(jnp.dot, preferred_element_type=F32)
    return dot(ah, bh) + (dot(ah, bl) + dot(al, bh))


def end_scalars(tile_read, along, rayleigh):
    tail = tile_read(2, 0)
    perp_w_zero = tile_read(2, 1)
    perp_w = tile_read(2, 2) - along * perp_w_zero
    gain = 1.0 / jnp.sqrt(tail + EPS)
    corner = gain * gain * perp_w
    couple = gain * perp_w_zero
    down, across = 2.0 * couple, rayleigh - corner
    most = jnp.maximum(jnp.abs(down), jnp.abs(across))
    safe = jnp.where(most > 0.0, most, 1.0)
    down, across = down / safe, jnp.where(most > 0.0, across / safe, 1.0)
    length = jnp.sqrt(down * down + across * across)
    larger = jnp.sqrt(0.5 * (1.0 + jnp.abs(across) / length))
    smaller = 0.5 * jnp.abs(down) / (length * larger)
    sign = jnp.where(down < 0.0, -1.0, 1.0)
    cosine = jnp.where(across >= 0.0, larger, smaller)
    sine = sign * jnp.where(across >= 0.0, smaller, larger)
    lam = sine * sine * rayleigh + cosine * cosine * corner - 2.0 * sine * cosine * couple
    return gain, sine, cosine, lam


def kernel(
    dims, sec, psi_hbm, left_hbm, right_hbm, den_hbm, source_ref, owner_ref, orders_ref,
    new_ref, corr_ref, *scratch
):
    far, near, core = dims
    chunks = psi_hbm.shape[0] // ROWS
    rows = psi_hbm.shape[0]
    width = psi_hbm.shape[2]
    op = far * near * core
    held = (scratch[:chunks], scratch[chunks : 2 * chunks])
    (left_f, right_f, left_h, left_l, right_h, right_l, inner, inner_h, inner_l, raw,
     applied, step, parts, got_core, got_near, got_far, picked, got_picked, chosen, psi_v, den_v, tiles, got_tiles, load_sem,
     gather_send, gather_recv, sum_send, sum_recv, tile_send, tile_recv) = scratch[2 * chunks :]

    me = lax.axis_index("op")
    y = lax.axis_index("sec")
    c = lax.rem(me, core)
    b = lax.rem(lax.div(me, core), near)
    a = lax.div(me, core * near)
    where = {"far": a, "near": b, "core": c, "sec": y}
    size = {"far": far, "near": near, "core": core, "sec": sec}

    def turned(axis, by):
        place = dict(where)
        place[axis] = lax.rem(where[axis] + by + size[axis], size[axis])
        return place

    def device(place):
        return ((place["far"] * near + place["near"]) * core + place["core"], place["sec"])

    every = [(axis, d) for axis in ("far", "near", "sec", "core") for d in range(1, size[axis])]
    around = [
        (("near", i), ("core", j), ("sec", l))
        for i in range(near) for j in range(core) for l in range(sec) if i + j + l > 0
    ]
    along_far = [(("far", d),) for d in range(1, far)]

    def moved(offset):
        place = dict(where)
        for axis, by in offset:
            place[axis] = lax.rem(where[axis] + by, size[axis])
        return place

    loads = [
        pltpu.make_async_copy(right_hbm, right_f, load_sem.at[0]),
        pltpu.make_async_copy(left_hbm, left_f, load_sem.at[1]),
        pltpu.make_async_copy(psi_hbm.at[:, 0], psi_v, load_sem.at[2]),
        pltpu.make_async_copy(den_hbm.at[:, 0], den_v, load_sem.at[3]),
    ]
    for n in (2, 0, 1, 3):
        loads[n].start()

    barrier = pltpu.get_barrier_semaphore()
    for offset in around + along_far:
        pl.semaphore_signal(
            barrier, inc=1, device_id=device(moved(offset)), device_id_type=MESH
        )

    sector = jnp.int32(0)
    for s in range(sec):
        sector = sector + jnp.where(owner_ref[s] == y, s, 0)
    order = orders_ref[sector]
    source = owner_ref[source_ref[me, sector]]

    row_ids = lax.broadcasted_iota(jnp.int32, (rows, width), 0) + me * rows
    col_ids = lax.broadcasted_iota(jnp.int32, (rows, width), 1)
    mask = ((row_ids < order) & (col_ids < order)).astype(F32)
    loads[2].wait()
    raw[...] = psi_v[...] * mask
    for k in range(chunks):
        held[0][k][y, a, b] = raw[pl.ds(k * ROWS, ROWS), :]

    pl.semaphore_wait(barrier, len(around + along_far))

    def area(axes, place):
        pick = lambda axis: slice(None) if axis in axes else place[axis]
        return (pick("sec"), pick("far"), pick("near"))

    def sequence(k):
        return ("far", "near", "sec") if k % 2 == 0 else ("far", "sec", "near")

    slot_of = {pair: n for n, pair in enumerate(every)}

    def gather_copy(turn, k, stage, d, from_place, to_place):
        axes = sequence(k)
        block = held[turn][k].at[area(axes[:stage], from_place)]
        n = slot_of[(axes[stage], d)]
        return pltpu.make_async_remote_copy(
            src_ref=block, dst_ref=block,
            send_sem=gather_send.at[turn, k, n], recv_sem=gather_recv.at[turn, k, n],
            device_id=device(to_place), device_id_type=MESH,
        )

    def gather_start(turn, k, stage):
        axis = sequence(k)[stage]
        for d in range(1, size[axis]):
            gather_copy(turn, k, stage, d, where, turned(axis, d)).start()

    def gather_wait(turn, k, stage):
        axis = sequence(k)[stage]
        for d in range(1, size[axis]):
            gather_copy(turn, k, stage, d, turned(axis, -d), turned(axis, d)).wait_recv()

    def pick_copy(turn, k, d):
        n = slot_of[("core", d)]
        return pltpu.make_async_remote_copy(
            src_ref=picked.at[turn, k, d - 1], dst_ref=got_picked.at[turn, k, d - 1],
            send_sem=gather_send.at[turn, k, n], recv_sem=gather_recv.at[turn, k, n],
            device_id=device(turned("core", d)), device_id_type=MESH,
        )

    def pick_start(turn, k):
        for d in range(1, core):
            term = me - c + lax.rem(c + d, core)
            picked[turn, k, d - 1] = held[turn][k][owner_ref[source_ref[term, sector]]]
            pick_copy(turn, k, d).start()

    def pick_wait(turn, k):
        chosen[:, :, c] = held[turn][k][source]
        for d in range(1, core):
            pick_copy(turn, k, d).wait_recv()
            chosen[:, :, lax.rem(c + core - d, core)] = got_picked[turn, k, d - 1]

    def gather_end(turn):
        for k in range(chunks):
            for d in range(1, core):
                pick_copy(turn, k, d).wait_send()
            for stage, axis in enumerate(sequence(k)):
                for d in range(1, size[axis]):
                    gather_copy(turn, k, stage, d, where, turned(axis, d)).wait_send()

    groups = (around, along_far)

    def tile_copy(red, stage, n):
        slot = n + stage * len(around)
        return pltpu.make_async_remote_copy(
            src_ref=tiles.at[red, stage], dst_ref=got_tiles.at[red, slot],
            send_sem=tile_send.at[red, slot], recv_sem=tile_recv.at[red, slot],
            device_id=device(moved(groups[stage][n])), device_id_type=MESH,
        )

    def tile_send_all(red, stage):
        for n in range(len(groups[stage])):
            tile_copy(red, stage, n).start()

    def tile_start(red, values):
        line = lax.broadcasted_iota(jnp.int32, (8, 128), 0)
        tile = jnp.zeros((8, 128), F32)
        for n, value in enumerate(values):
            tile = jnp.where(line == n, value, tile)
        tiles[red, 0] = tile
        tile_send_all(red, 0)

    def tile_advance(red, stage):
        total = tiles[red, stage]
        for n in range(len(groups[stage])):
            tile_copy(red, stage, n).wait_recv()
            total = total + got_tiles[red, n + stage * len(around)]
        tiles[red, stage + 1] = total
        if stage == 0:
            tile_send_all(red, 1)

    count = float(rows * width * op * sec)

    def tile_read(red, n):
        return tiles[red, 2, pl.ds(n, 1), pl.ds(0, 1)] / count

    def total(value):
        return jnp.sum(value.reshape(-1, width), keepdims=True)

    def core_copy(turn, k, d):
        place = turned("core", d)
        return pltpu.make_async_remote_copy(
            src_ref=parts.at[turn, k, :, :, place["core"]], dst_ref=got_core.at[turn, k, d - 1],
            send_sem=sum_send.at[turn, k, slot_of[("core", d)]],
            recv_sem=sum_recv.at[turn, k, slot_of[("core", d)]],
            device_id=device(place), device_id_type=MESH,
        )

    def near_copy(turn, k, d):
        place = turned("near", d)
        return pltpu.make_async_remote_copy(
            src_ref=parts.at[turn, k, :, place["near"], c], dst_ref=got_near.at[turn, k, d - 1],
            send_sem=sum_send.at[turn, k, slot_of[("near", d)]],
            recv_sem=sum_recv.at[turn, k, slot_of[("near", d)]],
            device_id=device(place), device_id_type=MESH,
        )

    def far_copy(turn, k, d):
        place = turned("far", d)
        return pltpu.make_async_remote_copy(
            src_ref=parts.at[turn, k, place["far"], b, c], dst_ref=got_far.at[turn, k, d - 1],
            send_sem=sum_send.at[turn, k, slot_of[("far", d)]],
            recv_sem=sum_recv.at[turn, k, slot_of[("far", d)]],
            device_id=device(place), device_id_type=MESH,
        )

    def sum_core(turn, k):
        for d in range(1, core):
            core_copy(turn, k, d).wait_recv()
        mine = parts[turn, k, :, :, c]
        for d in range(1, core):
            mine = mine + got_core[turn, k, d - 1]
        parts[turn, k, :, :, c] = mine
        for d in range(1, near):
            near_copy(turn, k, d).start()
        return mine

    def sum_near(turn, k):
        for d in range(1, near):
            near_copy(turn, k, d).wait_recv()
        mine = parts[turn, k, :, b, c]
        for d in range(1, near):
            mine = mine + got_near[turn, k, d - 1]
        parts[turn, k, :, b, c] = mine
        for d in range(1, far):
            far_copy(turn, k, d).start()

    def sum_far(turn, k):
        for d in range(1, far):
            far_copy(turn, k, d).wait_recv()
        mine = parts[turn, k, a, b, c]
        for d in range(1, far):
            mine = mine + got_far[turn, k, d - 1]
        return mine

    def sum_end(turn):
        for k in range(chunks):
            for n in range(1, core):
                core_copy(turn, k, n).wait_send()
            for n in range(1, near):
                near_copy(turn, k, n).wait_send()
            for n in range(1, far):
                far_copy(turn, k, n).wait_send()

    def gather_rest(turn, beside):
        for k in range(chunks + 1):
            if k < chunks:
                gather_wait(turn, k, 0)
                gather_start(turn, k, 1)
                beside(k)
            if k > 0:
                gather_wait(turn, k - 1, 1)
                gather_start(turn, k - 1, 2)

    def matmuls(turn, weigh):
        for k in range(chunks + 1):
            if k < chunks:
                gather_wait(turn, k, 2)
                pick_start(turn, k)
            if k > 0:
                pick_wait(turn, k - 1)
                high, low = split(chosen[...].reshape(op * ROWS, width))
                inner[:, pl.ds((k - 1) * ROWS, ROWS), :] = product3(
                    high, low, right_h[...], right_l[...]
                ).reshape(op, ROWS, width)
        whole = inner[...].reshape(op * rows, width)
        high, low = split(whole)
        inner_h[...] = high
        inner_l[...] = low
        weighed = jnp.zeros((1, 1), F32)
        for k in range(chunks):
            out = product3(left_h[k], left_l[k], inner_h[...], inner_l[...])
            parts[turn, k] = out.reshape(far, near, core, ROWS, width)
            for d in range(1, core):
                core_copy(turn, k, d).start()
            if k > 0:
                weighed = weighed + total(weigh(k - 1) * sum_core(turn, k - 1))
        return weighed + total(weigh(chunks - 1) * sum_core(turn, chunks - 1))

    def finish(turn, red, ready, use):
        values = None
        for k in range(chunks + 2):
            if k < chunks:
                sum_near(turn, k)
            if k < 2:
                tile_advance(red, k)
            else:
                if k == 2:
                    values = ready()
                use(k - 2, values)

    for k in range(chunks):
        gather_start(0, k, 0)
    loads[0].wait()
    high, low = split(right_f[...])
    right_h[...] = high
    right_l[...] = low
    norm_part = total(raw[...] * raw[...])
    loads[1].wait()
    loads[3].wait()

    def split_left(k):
        high, low = split(left_f[:, pl.ds(k * ROWS, ROWS), :].reshape(op * ROWS, width))
        left_h[k] = high
        left_l[k] = low

    gather_rest(0, split_left)
    start_part = matmuls(0, lambda k: held[0][k][y])
    tile_start(0, (norm_part, start_part))

    def start_values():
        norm_raw = tile_read(0, 0)
        product_raw = tile_read(0, 1)
        return 1.0 / jnp.sqrt(norm_raw + EPS), product_raw / (norm_raw + EPS)

    kept = {"along": jnp.zeros((1, 1), F32)}

    def take_step(k, values):
        scale, rayleigh = values
        kept["scale"], kept["rayleigh"] = values
        here = pl.ds(k * ROWS, ROWS)
        v_zero = scale * raw[here, :]
        w_zero = scale * (sum_far(0, k) * mask[k * ROWS : (k + 1) * ROWS])
        update = (w_zero - rayleigh * v_zero) / den_v[here, :]
        applied[here, :] = w_zero
        step[here, :] = update
        held[1][k][y, a, b] = update
        gather_start(1, k, 0)
        kept["along"] = kept["along"] + total(v_zero * update)

    finish(0, 0, start_values, take_step)
    scale, rayleigh = kept["scale"], kept["rayleigh"]

    tile_start(1, (kept["along"],))

    def sum_along(k):
        if k in (1, 3):
            tile_advance(1, k // 2)

    gather_rest(1, sum_along)
    for stage in range(2):
        if 2 * stage + 1 >= chunks:
            tile_advance(1, stage)
    along = tile_read(1, 0)
    v_zero = scale * raw[...]
    update_perp = step[...] - along * v_zero
    step[...] = update_perp
    tail_part = total(update_perp * update_perp)
    couple_part = total(update_perp * applied[...])
    shift = along * scale
    corner_part = matmuls(1, lambda k: held[1][k][y] - shift * held[0][k][y])
    tile_start(2, (tail_part, couple_part, corner_part))

    def end_values():
        return end_scalars(tile_read, along, rayleigh)

    def give(k, values):
        gain, sine, cosine, lam = values
        here = pl.ds(k * ROWS, ROWS)
        w_zero = applied[here, :]
        w_one = gain * (sum_far(1, k) * mask[k * ROWS : (k + 1) * ROWS] - along * w_zero)
        new_vector = sine * (scale * raw[here, :]) - cosine * (gain * step[here, :])
        mixed = sine * w_zero - cosine * w_one
        new_ref[here, :] = new_vector
        corr_ref[here, :] = (mixed - lam * new_vector) / den_v[here, :]

    finish(1, 2, end_values, give)

    for turn in range(2):
        gather_end(turn)
        sum_end(turn)
    for red in range(3):
        for stage in range(2):
            for n in range(len(groups[stage])):
                tile_copy(red, stage, n).wait_send()


def fused(dims, sec, psi, left_env, right_env, denominators, source_sector, owner, orders):
    rows, _, width = psi.shape
    far, near, core = dims
    op = far * near * core
    chunks = rows // ROWS
    peers = far + near + core + sec - 4
    pairs = near * core * sec - 1 + far - 1
    vmem = pl.BlockSpec(memory_space=pltpu.VMEM)
    smem = pl.BlockSpec(memory_space=pltpu.SMEM)
    hbm = pl.BlockSpec(memory_space=pl.ANY)
    block = (ROWS, width)
    scratch = [pltpu.VMEM((sec, far, near) + block, F32)] * (2 * chunks) + [
        pltpu.VMEM((op, rows, width), F32),
        pltpu.VMEM((width, width), F32),
        pltpu.VMEM((chunks, op * ROWS, width), BF16),
        pltpu.VMEM((chunks, op * ROWS, width), BF16),
        pltpu.VMEM((width, width), BF16),
        pltpu.VMEM((width, width), BF16),
        pltpu.VMEM((op, rows, width), F32),
        pltpu.VMEM((op * rows, width), BF16),
        pltpu.VMEM((op * rows, width), BF16),
        pltpu.VMEM((rows, width), F32),
        pltpu.VMEM((rows, width), F32),
        pltpu.VMEM((rows, width), F32),
        pltpu.VMEM((2, chunks, far, near, core) + block, F32),
        pltpu.VMEM((2, chunks, core - 1, far, near) + block, F32),
        pltpu.VMEM((2, chunks, near - 1, far) + block, F32),
        pltpu.VMEM((2, chunks, far - 1) + block, F32),
        pltpu.VMEM((2, chunks, core - 1, far, near) + block, F32),
        pltpu.VMEM((2, chunks, core - 1, far, near) + block, F32),
        pltpu.VMEM((far, near, core) + block, F32),
        pltpu.VMEM((rows, width), F32),
        pltpu.VMEM((rows, width), F32),
        pltpu.VMEM((3, 3, 8, 128), F32),
        pltpu.VMEM((3, pairs, 8, 128), F32),
        pltpu.SemaphoreType.DMA((4,)),
        pltpu.SemaphoreType.DMA((2, chunks, peers)),
        pltpu.SemaphoreType.DMA((2, chunks, peers)),
        pltpu.SemaphoreType.DMA((2, chunks, peers)),
        pltpu.SemaphoreType.DMA((2, chunks, peers)),
        pltpu.SemaphoreType.DMA((3, pairs)),
        pltpu.SemaphoreType.DMA((3, pairs)),
    ]
    flat = jax.ShapeDtypeStruct((rows, width), F32)
    new_vector, correction = pl.pallas_call(
        functools.partial(kernel, dims, sec),
        out_shape=(flat, flat),
        in_specs=[hbm, hbm, hbm, hbm, smem, smem, smem],
        out_specs=(vmem, vmem),
        scratch_shapes=scratch,
        compiler_params=pltpu.CompilerParams(
            collective_id=0, has_side_effects=True, vmem_limit_bytes=52 * 2**20
        ),
    )(
        psi,
        left_env.reshape(op, rows, width),
        right_env.reshape(width, width),
        denominators,
        source_sector,
        owner,
        orders,
    )
    return new_vector.reshape(psi.shape), correction.reshape(psi.shape)


def per_device(*arrays):
    psi, left_env = arrays[0], arrays[1]
    op = lax.axis_size("op")
    sec = lax.axis_size("sec")
    rows, sec_here, width = psi.shape
    core = 2 if op % 2 == 0 else 1
    chips = op // core
    near = max(n for n in range(1, chips + 1) if chips % n == 0 and n * n <= chips)
    dims = (chips // near, near, core)
    fits = rows % ROWS == 0 and width % 128 == 0 and left_env.shape[:2] == (1, 1)
    if fits and sec_here == 1 and min(dims) > 1 and sec > 1 and op * rows == width:
        return fused(dims, sec, *arrays)
    return general(*arrays)


def solution(mesh):
    placed = (
        P("op", "sec", None),
        P("op", "sec", None, None),
        P("op", "sec", None, None),
        P("op", "sec", None),
        P(),
        P(),
        P(),
    )
    return jax.shard_map(
        per_device,
        mesh=mesh,
        in_specs=placed,
        out_specs=(P("op", "sec", None), P("op", "sec", None)),
        check_vma=False,
    )
```

```python
import functools

import jax
import jax.numpy as jnp
from jax import lax
from jax.experimental import pallas as pl
from jax.experimental.pallas import tpu as pltpu
from jax.sharding import PartitionSpec as P

EPS = 1e-06
HIGH = lax.Precision.HIGHEST
MESH = pl.DeviceIdType.MESH
F32 = jnp.float32
BF16 = jnp.bfloat16
ROWS = 8


def slot_sectors(owner):
    slots = jnp.arange(owner.shape[0], dtype=jnp.int32)
    hits = (owner[None, :] == slots[:, None]).astype(jnp.int32)
    return jnp.sum(hits * slots[None, :], axis=1)


def general(psi, left_env, right_env, denominators, source_sector, owner, orders):
    rows_here = psi.shape[0]
    sec_here = psi.shape[1]
    width = psi.shape[2]
    term_here = left_env.shape[0]
    op_size = lax.axis_size("op")
    sec_size = lax.axis_size("sec")
    op_pos = lax.axis_index("op")
    sec_pos = lax.axis_index("sec")
    sectors = slot_sectors(owner)
    sectors_here = lax.dynamic_slice_in_dim(sectors, sec_pos * sec_here, sec_here, 0)
    order_here = jnp.take(orders, sectors_here)
    row_ids = op_pos * rows_here + jnp.arange(rows_here, dtype=jnp.int32)
    col_ids = jnp.arange(width, dtype=jnp.int32)
    mask = (
        (row_ids[:, None, None] < order_here[None, :, None])
        & (col_ids[None, None, :] < order_here[None, :, None])
    ).astype(jnp.float32)
    source_all = jnp.take(owner, jnp.take(source_sector, sectors_here, axis=1))
    blocks = term_here * sec_here
    left_flat = left_env.reshape(blocks, width, width)
    right_flat = right_env.reshape(blocks, width, width)
    count = float(rows_here * sec_here * width * op_size * sec_size)

    def apply(vector):
        shard_all = lax.all_gather(vector, "sec", axis=1, tiled=True)
        outgoing = jnp.take(shard_all, source_all.reshape(-1), axis=1).reshape(
            rows_here, op_size, blocks, width
        )
        chosen = lax.all_to_all(outgoing, "op", split_axis=1, concat_axis=0, tiled=True).reshape(
            width, blocks, width
        )
        inner = jnp.einsum("apb,pbc->apc", chosen, right_flat, precision=HIGH)
        product = jnp.einsum("pxa,apc->xpc", left_flat, inner, precision=HIGH)
        whole = product.reshape(width, term_here, sec_here, width).sum(axis=1)
        summed = lax.psum_scatter(whole, "op", scatter_dimension=0, tiled=True)
        return summed * mask

    def partial_sum(first, second):
        return jnp.sum(first * second)

    v_raw = psi * mask
    w_raw = apply(v_raw)
    start_pair = lax.psum(
        jnp.stack([partial_sum(v_raw, v_raw), partial_sum(v_raw, w_raw)]), ("op", "sec")
    )
    norm_raw = start_pair[0] / count
    product_raw = start_pair[1] / count
    scale = 1.0 / jnp.sqrt(norm_raw + EPS)
    v_zero = scale * v_raw
    w_zero = scale * w_raw
    rayleigh = product_raw / (norm_raw + EPS)
    update = (w_zero - rayleigh * v_zero) / denominators
    along = lax.psum(partial_sum(v_zero, update), ("op", "sec")) / count
    update_perp = update - along * v_zero
    tail = lax.psum(partial_sum(update_perp, update_perp), ("op", "sec")) / count
    v_one = update_perp / jnp.sqrt(tail + EPS)
    w_one = apply(v_one)
    sub_pair = lax.psum(
        jnp.stack([partial_sum(v_one, w_one), partial_sum(v_one, w_zero)]), ("op", "sec")
    )
    corner = sub_pair[0] / count
    couple = sub_pair[1] / count
    angle = 0.5 * jnp.arctan2(2.0 * couple, rayleigh - corner)
    sine = jnp.sin(angle)
    cosine = jnp.cos(angle)
    new_vector = sine * v_zero - cosine * v_one
    applied = sine * w_zero - cosine * w_one
    lam = sine * sine * rayleigh + cosine * cosine * corner - 2.0 * sine * cosine * couple
    correction = (applied - lam * new_vector) / denominators
    return (new_vector, correction)


def split(value):
    high = value.astype(BF16)
    return high, (value - high.astype(F32)).astype(BF16)


def product3(ah, al, bh, bl):
    dot = functools.partial(jnp.dot, preferred_element_type=F32)
    return dot(ah, bh) + (dot(ah, bl) + dot(al, bh))


def end_scalars(tile_read, along, rayleigh):
    tail = tile_read(2, 0)
    perp_w_zero = tile_read(2, 1)
    perp_w = tile_read(2, 2) - along * perp_w_zero
    gain = 1.0 / jnp.sqrt(tail + EPS)
    corner = gain * gain * perp_w
    couple = gain * perp_w_zero
    down, across = 2.0 * couple, rayleigh - corner
    most = jnp.maximum(jnp.abs(down), jnp.abs(across))
    safe = jnp.where(most > 0.0, most, 1.0)
    down, across = down / safe, jnp.where(most > 0.0, across / safe, 1.0)
    length = jnp.sqrt(down * down + across * across)
    larger = jnp.sqrt(0.5 * (1.0 + jnp.abs(across) / length))
    smaller = 0.5 * jnp.abs(down) / (length * larger)
    sign = jnp.where(down < 0.0, -1.0, 1.0)
    cosine = jnp.where(across >= 0.0, larger, smaller)
    sine = sign * jnp.where(across >= 0.0, smaller, larger)
    lam = sine * sine * rayleigh + cosine * cosine * corner - 2.0 * sine * cosine * couple
    return gain, sine, cosine, lam


def kernel(
    dims, sec, psi_hbm, left_hbm, right_hbm, den_hbm, source_ref, owner_ref, orders_ref,
    new_ref, corr_ref, *scratch
):
    far, near, core = dims
    chunks = psi_hbm.shape[0] // ROWS
    rows = psi_hbm.shape[0]
    width = psi_hbm.shape[2]
    op = far * near * core
    held = (scratch[:chunks], scratch[chunks : 2 * chunks])
    (left_f, right_f, left_h, left_l, right_h, right_l, inner, inner_h, inner_l, raw,
     applied, step, parts, got_core, got_near, got_far, picked, got_picked, chosen, psi_v, den_v, tiles, got_tiles, load_sem,
     gather_send, gather_recv, sum_send, sum_recv, tile_send, tile_recv) = scratch[2 * chunks :]

    me = lax.axis_index("op")
    y = lax.axis_index("sec")
    c = lax.rem(me, core)
    b = lax.rem(lax.div(me, core), near)
    a = lax.div(me, core * near)
    where = {"far": a, "near": b, "core": c, "sec": y}
    size = {"far": far, "near": near, "core": core, "sec": sec}

    def turned(axis, by):
        place = dict(where)
        place[axis] = lax.rem(where[axis] + by + size[axis], size[axis])
        return place

    def device(place):
        return ((place["far"] * near + place["near"]) * core + place["core"], place["sec"])

    every = [(axis, d) for axis in ("far", "near", "sec", "core") for d in range(1, size[axis])]
    around = [
        (("near", i), ("core", j), ("sec", l))
        for i in range(near) for j in range(core) for l in range(sec) if i + j + l > 0
    ]
    along_far = [(("far", d),) for d in range(1, far)]

    def moved(offset):
        place = dict(where)
        for axis, by in offset:
            place[axis] = lax.rem(where[axis] + by, size[axis])
        return place

    loads = [
        pltpu.make_async_copy(right_hbm, right_f, load_sem.at[0]),
        pltpu.make_async_copy(left_hbm, left_f, load_sem.at[1]),
        pltpu.make_async_copy(psi_hbm.at[:, 0], psi_v, load_sem.at[2]),
        pltpu.make_async_copy(den_hbm.at[:, 0], den_v, load_sem.at[3]),
    ]
    for n in (2, 0, 1, 3):
        loads[n].start()

    barrier = pltpu.get_barrier_semaphore()
    for offset in around + along_far:
        pl.semaphore_signal(
            barrier, inc=1, device_id=device(moved(offset)), device_id_type=MESH
        )

    sector = jnp.int32(0)
    for s in range(sec):
        sector = sector + jnp.where(owner_ref[s] == y, s, 0)
    order = orders_ref[sector]
    source = owner_ref[source_ref[me, sector]]

    row_ids = lax.broadcasted_iota(jnp.int32, (rows, width), 0) + me * rows
    col_ids = lax.broadcasted_iota(jnp.int32, (rows, width), 1)
    mask = ((row_ids < order) & (col_ids < order)).astype(F32)
    loads[2].wait()
    raw[...] = psi_v[...] * mask
    for k in range(chunks):
        held[0][k][y, a, b] = raw[pl.ds(k * ROWS, ROWS), :]

    pl.semaphore_wait(barrier, len(around + along_far))

    def area(axes, place):
        pick = lambda axis: slice(None) if axis in axes else place[axis]
        return (pick("sec"), pick("far"), pick("near"))

    def sequence(k):
        if k % 5 == 4:
            return ("near", "sec", "far")
        return ("far", "near", "sec") if k % 2 == 0 else ("far", "sec", "near")

    slot_of = {pair: n for n, pair in enumerate(every)}

    def gather_copy(turn, k, stage, d, from_place, to_place):
        axes = sequence(k)
        block = held[turn][k].at[area(axes[:stage], from_place)]
        n = slot_of[(axes[stage], d)]
        return pltpu.make_async_remote_copy(
            src_ref=block, dst_ref=block,
            send_sem=gather_send.at[turn, k, n], recv_sem=gather_recv.at[turn, k, n],
            device_id=device(to_place), device_id_type=MESH,
        )

    def gather_start(turn, k, stage):
        axis = sequence(k)[stage]
        for d in range(1, size[axis]):
            gather_copy(turn, k, stage, d, where, turned(axis, d)).start()

    def gather_wait(turn, k, stage):
        axis = sequence(k)[stage]
        for d in range(1, size[axis]):
            gather_copy(turn, k, stage, d, turned(axis, -d), turned(axis, d)).wait_recv()

    def pick_copy(turn, k, d):
        n = slot_of[("core", d)]
        return pltpu.make_async_remote_copy(
            src_ref=picked.at[turn, k, d - 1], dst_ref=got_picked.at[turn, k, d - 1],
            send_sem=gather_send.at[turn, k, n], recv_sem=gather_recv.at[turn, k, n],
            device_id=device(turned("core", d)), device_id_type=MESH,
        )

    def pick_start(turn, k):
        for d in range(1, core):
            term = me - c + lax.rem(c + d, core)
            picked[turn, k, d - 1] = held[turn][k][owner_ref[source_ref[term, sector]]]
            pick_copy(turn, k, d).start()

    def pick_wait(turn, k):
        chosen[:, :, c] = held[turn][k][source]
        for d in range(1, core):
            pick_copy(turn, k, d).wait_recv()
            chosen[:, :, lax.rem(c + core - d, core)] = got_picked[turn, k, d - 1]

    def gather_end(turn):
        for k in range(chunks):
            for d in range(1, core):
                pick_copy(turn, k, d).wait_send()
            for stage, axis in enumerate(sequence(k)):
                for d in range(1, size[axis]):
                    gather_copy(turn, k, stage, d, where, turned(axis, d)).wait_send()

    groups = (around, along_far)

    def tile_copy(red, stage, n):
        slot = n + stage * len(around)
        return pltpu.make_async_remote_copy(
            src_ref=tiles.at[red, stage], dst_ref=got_tiles.at[red, slot],
            send_sem=tile_send.at[red, slot], recv_sem=tile_recv.at[red, slot],
            device_id=device(moved(groups[stage][n])), device_id_type=MESH,
        )

    def tile_send_all(red, stage):
        for n in range(len(groups[stage])):
            tile_copy(red, stage, n).start()

    def tile_start(red, values):
        line = lax.broadcasted_iota(jnp.int32, (8, 128), 0)
        tile = jnp.zeros((8, 128), F32)
        for n, value in enumerate(values):
            tile = jnp.where(line == n, value, tile)
        tiles[red, 0] = tile
        tile_send_all(red, 0)

    def tile_advance(red, stage):
        total = tiles[red, stage]
        for n in range(len(groups[stage])):
            tile_copy(red, stage, n).wait_recv()
            total = total + got_tiles[red, n + stage * len(around)]
        tiles[red, stage + 1] = total
        if stage == 0:
            tile_send_all(red, 1)

    count = float(rows * width * op * sec)

    def tile_read(red, n):
        return tiles[red, 2, pl.ds(n, 1), pl.ds(0, 1)] / count

    def total(value):
        return jnp.sum(value.reshape(-1, width), keepdims=True)

    def core_copy(turn, k, d):
        place = turned("core", d)
        return pltpu.make_async_remote_copy(
            src_ref=parts.at[turn, k, :, :, place["core"]], dst_ref=got_core.at[turn, k, d - 1],
            send_sem=sum_send.at[turn, k, slot_of[("core", d)]],
            recv_sem=sum_recv.at[turn, k, slot_of[("core", d)]],
            device_id=device(place), device_id_type=MESH,
        )

    def sum_axes(k):
        return ("near", "far") if k % 2 == 0 else ("far", "near")

    def sum_copy(turn, k, stage, d):
        axis = sum_axes(k)[stage]
        place = turned(axis, d)
        if axis == "near":
            row = slice(None) if stage == 0 else a
            source_ref, target_ref = parts.at[turn, k, row, place["near"], c], got_near
        else:
            row = slice(None) if stage == 0 else b
            source_ref, target_ref = parts.at[turn, k, place["far"], row, c], got_far
        target = (turn, k, d - 1) if stage == 0 else (turn, k, d - 1, 0)
        return pltpu.make_async_remote_copy(
            src_ref=source_ref, dst_ref=target_ref.at[target],
            send_sem=sum_send.at[turn, k, slot_of[(axis, d)]],
            recv_sem=sum_recv.at[turn, k, slot_of[(axis, d)]],
            device_id=device(place), device_id_type=MESH,
        )

    def sum_core(turn, k):
        for d in range(1, core):
            core_copy(turn, k, d).wait_recv()
        mine = parts[turn, k, :, :, c]
        for d in range(1, core):
            mine = mine + got_core[turn, k, d - 1]
        parts[turn, k, :, :, c] = mine
        for d in range(1, size[sum_axes(k)[0]]):
            sum_copy(turn, k, 0, d).start()
        return mine

    def sum_first(turn, k):
        first, second = sum_axes(k)
        got = got_near if first == "near" else got_far
        index = (turn, k, slice(None), b, c) if first == "near" else (turn, k, a, slice(None), c)
        mine = parts[index]
        for d in range(1, size[first]):
            sum_copy(turn, k, 0, d).wait_recv()
            mine = mine + got[turn, k, d - 1]
        parts[index] = mine
        for d in range(1, size[second]):
            sum_copy(turn, k, 1, d).start()

    def sum_second(turn, k):
        second = sum_axes(k)[1]
        got = got_near if second == "near" else got_far
        mine = parts[turn, k, a, b, c]
        for d in range(1, size[second]):
            sum_copy(turn, k, 1, d).wait_recv()
            mine = mine + got[turn, k, d - 1, 0]
        return mine

    def sum_end(turn):
        for k in range(chunks):
            for n in range(1, core):
                core_copy(turn, k, n).wait_send()
            for stage, axis in enumerate(sum_axes(k)):
                for n in range(1, size[axis]):
                    sum_copy(turn, k, stage, n).wait_send()

    def gather_rest(turn, beside):
        for k in range(chunks + 1):
            if k < chunks:
                gather_wait(turn, k, 0)
                gather_start(turn, k, 1)
                beside(k)
            if k > 0:
                gather_wait(turn, k - 1, 1)
                gather_start(turn, k - 1, 2)

    def matmuls(turn, weigh):
        for k in range(chunks + 1):
            if k < chunks:
                gather_wait(turn, k, 2)
                pick_start(turn, k)
            if k > 0:
                pick_wait(turn, k - 1)
                high, low = split(chosen[...].reshape(op * ROWS, width))
                inner[:, pl.ds((k - 1) * ROWS, ROWS), :] = product3(
                    high, low, right_h[...], right_l[...]
                ).reshape(op, ROWS, width)
        whole = inner[...].reshape(op * rows, width)
        high, low = split(whole)
        inner_h[...] = high
        inner_l[...] = low
        weighed = jnp.zeros((1, 1), F32)
        for k in range(chunks):
            out = product3(left_h[k], left_l[k], inner_h[...], inner_l[...])
            parts[turn, k] = out.reshape(far, near, core, ROWS, width)
            for d in range(1, core):
                core_copy(turn, k, d).start()
            if k > 0:
                weighed = weighed + total(weigh(k - 1) * sum_core(turn, k - 1))
        return weighed + total(weigh(chunks - 1) * sum_core(turn, chunks - 1))

    def finish(turn, red, ready, use):
        values = None
        for k in range(chunks + 2):
            if k < chunks:
                sum_first(turn, k)
            if k < 2:
                tile_advance(red, k)
            else:
                if k == 2:
                    values = ready()
                use(k - 2, values)

    for k in range(chunks):
        gather_start(0, k, 0)
    loads[0].wait()
    high, low = split(right_f[...])
    right_h[...] = high
    right_l[...] = low
    norm_part = total(raw[...] * raw[...])
    loads[1].wait()
    loads[3].wait()

    def split_left(k):
        high, low = split(left_f[:, pl.ds(k * ROWS, ROWS), :].reshape(op * ROWS, width))
        left_h[k] = high
        left_l[k] = low

    gather_rest(0, split_left)
    start_part = matmuls(0, lambda k: held[0][k][y])
    tile_start(0, (norm_part, start_part))

    def start_values():
        norm_raw = tile_read(0, 0)
        product_raw = tile_read(0, 1)
        return 1.0 / jnp.sqrt(norm_raw + EPS), product_raw / (norm_raw + EPS)

    kept = {"along": jnp.zeros((1, 1), F32)}

    def take_step(k, values):
        scale, rayleigh = values
        kept["scale"], kept["rayleigh"] = values
        here = pl.ds(k * ROWS, ROWS)
        v_zero = scale * raw[here, :]
        w_zero = scale * (sum_second(0, k) * mask[k * ROWS : (k + 1) * ROWS])
        update = (w_zero - rayleigh * v_zero) / den_v[here, :]
        applied[here, :] = w_zero
        step[here, :] = update
        held[1][k][y, a, b] = update
        gather_start(1, k, 0)
        kept["along"] = kept["along"] + total(v_zero * update)

    finish(0, 0, start_values, take_step)
    scale, rayleigh = kept["scale"], kept["rayleigh"]

    tile_start(1, (kept["along"],))

    def sum_along(k):
        if k in (1, 3):
            tile_advance(1, k // 2)

    gather_rest(1, sum_along)
    for stage in range(2):
        if 2 * stage + 1 >= chunks:
            tile_advance(1, stage)
    along = tile_read(1, 0)
    v_zero = scale * raw[...]
    update_perp = step[...] - along * v_zero
    step[...] = update_perp
    tail_part = total(update_perp * update_perp)
    couple_part = total(update_perp * applied[...])
    shift = along * scale
    corner_part = matmuls(1, lambda k: held[1][k][y] - shift * held[0][k][y])
    tile_start(2, (tail_part, couple_part, corner_part))

    def end_values():
        return end_scalars(tile_read, along, rayleigh)

    def give(k, values):
        gain, sine, cosine, lam = values
        here = pl.ds(k * ROWS, ROWS)
        w_zero = applied[here, :]
        w_one = gain * (sum_second(1, k) * mask[k * ROWS : (k + 1) * ROWS] - along * w_zero)
        new_vector = sine * (scale * raw[here, :]) - cosine * (gain * step[here, :])
        mixed = sine * w_zero - cosine * w_one
        new_ref[here, :] = new_vector
        corr_ref[here, :] = (mixed - lam * new_vector) / den_v[here, :]

    finish(1, 2, end_values, give)

    for turn in range(2):
        gather_end(turn)
        sum_end(turn)
    for red in range(3):
        for stage in range(2):
            for n in range(len(groups[stage])):
                tile_copy(red, stage, n).wait_send()


def fused(dims, sec, psi, left_env, right_env, denominators, source_sector, owner, orders):
    rows, _, width = psi.shape
    far, near, core = dims
    op = far * near * core
    chunks = rows // ROWS
    peers = far + near + core + sec - 4
    pairs = near * core * sec - 1 + far - 1
    vmem = pl.BlockSpec(memory_space=pltpu.VMEM)
    smem = pl.BlockSpec(memory_space=pltpu.SMEM)
    hbm = pl.BlockSpec(memory_space=pl.ANY)
    block = (ROWS, width)
    scratch = [pltpu.VMEM((sec, far, near) + block, F32)] * (2 * chunks) + [
        pltpu.VMEM((op, rows, width), F32),
        pltpu.VMEM((width, width), F32),
        pltpu.VMEM((chunks, op * ROWS, width), BF16),
        pltpu.VMEM((chunks, op * ROWS, width), BF16),
        pltpu.VMEM((width, width), BF16),
        pltpu.VMEM((width, width), BF16),
        pltpu.VMEM((op, rows, width), F32),
        pltpu.VMEM((op * rows, width), BF16),
        pltpu.VMEM((op * rows, width), BF16),
        pltpu.VMEM((rows, width), F32),
        pltpu.VMEM((rows, width), F32),
        pltpu.VMEM((rows, width), F32),
        pltpu.VMEM((2, chunks, far, near, core) + block, F32),
        pltpu.VMEM((2, chunks, core - 1, far, near) + block, F32),
        pltpu.VMEM((2, chunks, near - 1, far) + block, F32),
        pltpu.VMEM((2, chunks, far - 1, near) + block, F32),
        pltpu.VMEM((2, chunks, core - 1, far, near) + block, F32),
        pltpu.VMEM((2, chunks, core - 1, far, near) + block, F32),
        pltpu.VMEM((far, near, core) + block, F32),
        pltpu.VMEM((rows, width), F32),
        pltpu.VMEM((rows, width), F32),
        pltpu.VMEM((3, 3, 8, 128), F32),
        pltpu.VMEM((3, pairs, 8, 128), F32),
        pltpu.SemaphoreType.DMA((4,)),
        pltpu.SemaphoreType.DMA((2, chunks, peers)),
        pltpu.SemaphoreType.DMA((2, chunks, peers)),
        pltpu.SemaphoreType.DMA((2, chunks, peers)),
        pltpu.SemaphoreType.DMA((2, chunks, peers)),
        pltpu.SemaphoreType.DMA((3, pairs)),
        pltpu.SemaphoreType.DMA((3, pairs)),
    ]
    flat = jax.ShapeDtypeStruct((rows, width), F32)
    new_vector, correction = pl.pallas_call(
        functools.partial(kernel, dims, sec),
        out_shape=(flat, flat),
        in_specs=[hbm, hbm, hbm, hbm, smem, smem, smem],
        out_specs=(vmem, vmem),
        scratch_shapes=scratch,
        compiler_params=pltpu.CompilerParams(
            collective_id=0, has_side_effects=True, vmem_limit_bytes=52 * 2**20
        ),
    )(
        psi,
        left_env.reshape(op, rows, width),
        right_env.reshape(width, width),
        denominators,
        source_sector,
        owner,
        orders,
    )
    return new_vector.reshape(psi.shape), correction.reshape(psi.shape)


def per_device(*arrays):
    psi, left_env = arrays[0], arrays[1]
    op = lax.axis_size("op")
    sec = lax.axis_size("sec")
    rows, sec_here, width = psi.shape
    core = 2 if op % 2 == 0 else 1
    chips = op // core
    near = max(n for n in range(1, chips + 1) if chips % n == 0 and n * n <= chips)
    dims = (chips // near, near, core)
    fits = rows % ROWS == 0 and width % 128 == 0 and left_env.shape[:2] == (1, 1)
    if fits and sec_here == 1 and min(dims) > 1 and sec > 1 and op * rows == width:
        return fused(dims, sec, *arrays)
    return general(*arrays)


def solution(mesh):
    placed = (
        P("op", "sec", None),
        P("op", "sec", None, None),
        P("op", "sec", None, None),
        P("op", "sec", None),
        P(),
        P(),
        P(),
    )
    return jax.shard_map(
        per_device,
        mesh=mesh,
        in_specs=placed,
        out_specs=(P("op", "sec", None), P("op", "sec", None)),
        check_vma=False,
    )
```

```python
import functools

import jax
import jax.numpy as jnp
from jax import lax
from jax.experimental import pallas as pl
from jax.experimental.pallas import tpu as pltpu
from jax.sharding import PartitionSpec as P

EPS = 1e-06
HIGH = lax.Precision.HIGHEST
MESH = pl.DeviceIdType.MESH
F32 = jnp.float32
BF16 = jnp.bfloat16
ROWS = 8
TILE = 256


def slot_sectors(owner):
    slots = jnp.arange(owner.shape[0], dtype=jnp.int32)
    hits = (owner[None, :] == slots[:, None]).astype(jnp.int32)
    return jnp.sum(hits * slots[None, :], axis=1)


def general(psi, left_env, right_env, denominators, source_sector, owner, orders):
    rows_here = psi.shape[0]
    sec_here = psi.shape[1]
    width = psi.shape[2]
    term_here = left_env.shape[0]
    op_size = lax.axis_size("op")
    sec_size = lax.axis_size("sec")
    op_pos = lax.axis_index("op")
    sec_pos = lax.axis_index("sec")
    sectors = slot_sectors(owner)
    sectors_here = lax.dynamic_slice_in_dim(sectors, sec_pos * sec_here, sec_here, 0)
    order_here = jnp.take(orders, sectors_here)
    row_ids = op_pos * rows_here + jnp.arange(rows_here, dtype=jnp.int32)
    col_ids = jnp.arange(width, dtype=jnp.int32)
    mask = (
        (row_ids[:, None, None] < order_here[None, :, None])
        & (col_ids[None, None, :] < order_here[None, :, None])
    ).astype(jnp.float32)
    source_all = jnp.take(owner, jnp.take(source_sector, sectors_here, axis=1))
    blocks = term_here * sec_here
    left_flat = left_env.reshape(blocks, width, width)
    right_flat = right_env.reshape(blocks, width, width)
    count = float(rows_here * sec_here * width * op_size * sec_size)

    def apply(vector):
        shard_all = lax.all_gather(vector, "sec", axis=1, tiled=True)
        outgoing = jnp.take(shard_all, source_all.reshape(-1), axis=1).reshape(
            rows_here, op_size, blocks, width
        )
        chosen = lax.all_to_all(outgoing, "op", split_axis=1, concat_axis=0, tiled=True).reshape(
            width, blocks, width
        )
        inner = jnp.einsum("apb,pbc->apc", chosen, right_flat, precision=HIGH)
        product = jnp.einsum("pxa,apc->xpc", left_flat, inner, precision=HIGH)
        whole = product.reshape(width, term_here, sec_here, width).sum(axis=1)
        summed = lax.psum_scatter(whole, "op", scatter_dimension=0, tiled=True)
        return summed * mask

    def partial_sum(first, second):
        return jnp.sum(first * second)

    v_raw = psi * mask
    w_raw = apply(v_raw)
    start_pair = lax.psum(
        jnp.stack([partial_sum(v_raw, v_raw), partial_sum(v_raw, w_raw)]), ("op", "sec")
    )
    norm_raw = start_pair[0] / count
    product_raw = start_pair[1] / count
    scale = 1.0 / jnp.sqrt(norm_raw + EPS)
    v_zero = scale * v_raw
    w_zero = scale * w_raw
    rayleigh = product_raw / (norm_raw + EPS)
    update = (w_zero - rayleigh * v_zero) / denominators
    along = lax.psum(partial_sum(v_zero, update), ("op", "sec")) / count
    update_perp = update - along * v_zero
    tail = lax.psum(partial_sum(update_perp, update_perp), ("op", "sec")) / count
    v_one = update_perp / jnp.sqrt(tail + EPS)
    w_one = apply(v_one)
    sub_pair = lax.psum(
        jnp.stack([partial_sum(v_one, w_one), partial_sum(v_one, w_zero)]), ("op", "sec")
    )
    corner = sub_pair[0] / count
    couple = sub_pair[1] / count
    angle = 0.5 * jnp.arctan2(2.0 * couple, rayleigh - corner)
    sine = jnp.sin(angle)
    cosine = jnp.cos(angle)
    new_vector = sine * v_zero - cosine * v_one
    applied = sine * w_zero - cosine * w_one
    lam = sine * sine * rayleigh + cosine * cosine * corner - 2.0 * sine * cosine * couple
    correction = (applied - lam * new_vector) / denominators
    return (new_vector, correction)


def split(value):
    high = value.astype(BF16)
    return high, (value - high.astype(F32)).astype(BF16)


def product3(ah, al, bh, bl):
    dot = functools.partial(jnp.dot, preferred_element_type=F32)
    return dot(ah, bh) + (dot(ah, bl) + dot(al, bh))


def end_scalars(tile_read, along, rayleigh):
    tail = tile_read(2, 0)
    perp_w_zero = tile_read(2, 1)
    perp_w = tile_read(2, 2) - along * perp_w_zero
    gain = 1.0 / jnp.sqrt(tail + EPS)
    corner = gain * gain * perp_w
    couple = gain * perp_w_zero
    down, across = 2.0 * couple, rayleigh - corner
    most = jnp.maximum(jnp.abs(down), jnp.abs(across))
    safe = jnp.where(most > 0.0, most, 1.0)
    down, across = down / safe, jnp.where(most > 0.0, across / safe, 1.0)
    length = jnp.sqrt(down * down + across * across)
    larger = jnp.sqrt(0.5 * (1.0 + jnp.abs(across) / length))
    smaller = 0.5 * jnp.abs(down) / (length * larger)
    sign = jnp.where(down < 0.0, -1.0, 1.0)
    cosine = jnp.where(across >= 0.0, larger, smaller)
    sine = sign * jnp.where(across >= 0.0, smaller, larger)
    lam = sine * sine * rayleigh + cosine * cosine * corner - 2.0 * sine * cosine * couple
    return gain, sine, cosine, lam


def kernel(
    dims, sec, psi_hbm, left_hbm, right_hbm, den_hbm, source_ref, owner_ref, orders_ref,
    new_ref, corr_ref, *scratch
):
    far, near, core = dims
    chunks = psi_hbm.shape[0] // ROWS
    rows = psi_hbm.shape[0]
    width = psi_hbm.shape[2]
    op = far * near * core
    held = (scratch[:chunks], scratch[chunks : 2 * chunks])
    (left_f, right_f, left_h, left_l, right_h, right_l, inner, vector_h, vector_l, inner_h, inner_l, raw,
     applied, step, parts, got_core, got_near, got_far, picked, got_picked, chosen, psi_v, den_v, tiles, got_tiles, load_sem,
     gather_send, gather_recv, sum_send, sum_recv, tile_send, tile_recv) = scratch[2 * chunks :]

    me = lax.axis_index("op")
    y = lax.axis_index("sec")
    c = lax.rem(me, core)
    b = lax.rem(lax.div(me, core), near)
    a = lax.div(me, core * near)
    where = {"far": a, "near": b, "core": c, "sec": y}
    size = {"far": far, "near": near, "core": core, "sec": sec}

    def turned(axis, by):
        place = dict(where)
        place[axis] = lax.rem(where[axis] + by + size[axis], size[axis])
        return place

    def device(place):
        return ((place["far"] * near + place["near"]) * core + place["core"], place["sec"])

    every = [(axis, d) for axis in ("far", "near", "sec", "core") for d in range(1, size[axis])]
    around = [
        (("near", i), ("core", j), ("sec", l))
        for i in range(near) for j in range(core) for l in range(sec) if i + j + l > 0
    ]
    along_far = [(("far", d),) for d in range(1, far)]

    def moved(offset):
        place = dict(where)
        for axis, by in offset:
            place[axis] = lax.rem(where[axis] + by, size[axis])
        return place

    loads = [
        pltpu.make_async_copy(right_hbm, right_f, load_sem.at[0]),
        pltpu.make_async_copy(left_hbm, left_f, load_sem.at[1]),
        pltpu.make_async_copy(psi_hbm.at[:, 0], psi_v, load_sem.at[2]),
        pltpu.make_async_copy(den_hbm.at[:, 0], den_v, load_sem.at[3]),
    ]
    for n in (2, 0, 1, 3):
        loads[n].start()

    barrier = pltpu.get_barrier_semaphore()
    for offset in around + along_far:
        pl.semaphore_signal(
            barrier, inc=1, device_id=device(moved(offset)), device_id_type=MESH
        )

    sector = jnp.int32(0)
    for s in range(sec):
        sector = sector + jnp.where(owner_ref[s] == y, s, 0)
    order = orders_ref[sector]
    source = owner_ref[source_ref[me, sector]]

    row_ids = lax.broadcasted_iota(jnp.int32, (rows, width), 0) + me * rows
    col_ids = lax.broadcasted_iota(jnp.int32, (rows, width), 1)
    mask = ((row_ids < order) & (col_ids < order)).astype(F32)
    loads[2].wait()
    raw[...] = psi_v[...] * mask
    for k in range(chunks):
        held[0][k][y, a, b] = raw[pl.ds(k * ROWS, ROWS), :]

    pl.semaphore_wait(barrier, len(around + along_far))

    def area(axes, place):
        pick = lambda axis: slice(None) if axis in axes else place[axis]
        return (pick("sec"), pick("far"), pick("near"))

    def sequence(k):
        if k % 5 == 4:
            return ("near", "sec", "far")
        return ("far", "near", "sec") if k % 2 == 0 else ("far", "sec", "near")

    slot_of = {pair: n for n, pair in enumerate(every)}

    def gather_copy(turn, k, stage, d, from_place, to_place):
        axes = sequence(k)
        block = held[turn][k].at[area(axes[:stage], from_place)]
        n = slot_of[(axes[stage], d)]
        return pltpu.make_async_remote_copy(
            src_ref=block, dst_ref=block,
            send_sem=gather_send.at[turn, k, n], recv_sem=gather_recv.at[turn, k, n],
            device_id=device(to_place), device_id_type=MESH,
        )

    def gather_start(turn, k, stage):
        axis = sequence(k)[stage]
        for d in range(1, size[axis]):
            gather_copy(turn, k, stage, d, where, turned(axis, d)).start()

    def gather_wait(turn, k, stage):
        axis = sequence(k)[stage]
        for d in range(1, size[axis]):
            gather_copy(turn, k, stage, d, turned(axis, -d), turned(axis, d)).wait_recv()

    def pick_copy(turn, k, d):
        n = slot_of[("core", d)]
        return pltpu.make_async_remote_copy(
            src_ref=picked.at[turn, k, d - 1], dst_ref=got_picked.at[turn, k, d - 1],
            send_sem=gather_send.at[turn, k, n], recv_sem=gather_recv.at[turn, k, n],
            device_id=device(turned("core", d)), device_id_type=MESH,
        )

    def pick_start(turn, k):
        for d in range(1, core):
            term = me - c + lax.rem(c + d, core)
            picked[turn, k, d - 1] = held[turn][k][owner_ref[source_ref[term, sector]]]
            pick_copy(turn, k, d).start()

    def pick_wait(turn, k):
        chosen[:, :, c] = held[turn][k][source]
        for d in range(1, core):
            pick_copy(turn, k, d).wait_recv()
            chosen[:, :, lax.rem(c + core - d, core)] = got_picked[turn, k, d - 1]

    def gather_end(turn):
        for k in range(chunks):
            for d in range(1, core):
                pick_copy(turn, k, d).wait_send()
            for stage, axis in enumerate(sequence(k)):
                for d in range(1, size[axis]):
                    gather_copy(turn, k, stage, d, where, turned(axis, d)).wait_send()

    groups = (around, along_far)

    def tile_copy(red, stage, n):
        slot = n + stage * len(around)
        return pltpu.make_async_remote_copy(
            src_ref=tiles.at[red, stage], dst_ref=got_tiles.at[red, slot],
            send_sem=tile_send.at[red, slot], recv_sem=tile_recv.at[red, slot],
            device_id=device(moved(groups[stage][n])), device_id_type=MESH,
        )

    def tile_send_all(red, stage):
        for n in range(len(groups[stage])):
            tile_copy(red, stage, n).start()

    def tile_start(red, values):
        line = lax.broadcasted_iota(jnp.int32, (8, 128), 0)
        tile = jnp.zeros((8, 128), F32)
        for n, value in enumerate(values):
            tile = jnp.where(line == n, value, tile)
        tiles[red, 0] = tile
        tile_send_all(red, 0)

    def tile_advance(red, stage):
        total = tiles[red, stage]
        for n in range(len(groups[stage])):
            tile_copy(red, stage, n).wait_recv()
            total = total + got_tiles[red, n + stage * len(around)]
        tiles[red, stage + 1] = total
        if stage == 0:
            tile_send_all(red, 1)

    count = float(rows * width * op * sec)

    def tile_read(red, n):
        return tiles[red, 2, pl.ds(n, 1), pl.ds(0, 1)] / count

    def total(value):
        return jnp.sum(value.reshape(-1, width), keepdims=True)

    def core_copy(turn, k, d):
        place = turned("core", d)
        return pltpu.make_async_remote_copy(
            src_ref=parts.at[turn, k, :, :, place["core"]], dst_ref=got_core.at[turn, k, d - 1],
            send_sem=sum_send.at[turn, k, slot_of[("core", d)]],
            recv_sem=sum_recv.at[turn, k, slot_of[("core", d)]],
            device_id=device(place), device_id_type=MESH,
        )

    def sum_axes(k):
        return ("near", "far") if k % 2 == 0 else ("far", "near")

    def sum_copy(turn, k, stage, d):
        axis = sum_axes(k)[stage]
        place = turned(axis, d)
        if axis == "near":
            row = slice(None) if stage == 0 else a
            source_ref, target_ref = parts.at[turn, k, row, place["near"], c], got_near
        else:
            row = slice(None) if stage == 0 else b
            source_ref, target_ref = parts.at[turn, k, place["far"], row, c], got_far
        target = (turn, k, d - 1) if stage == 0 else (turn, k, d - 1, 0)
        return pltpu.make_async_remote_copy(
            src_ref=source_ref, dst_ref=target_ref.at[target],
            send_sem=sum_send.at[turn, k, slot_of[(axis, d)]],
            recv_sem=sum_recv.at[turn, k, slot_of[(axis, d)]],
            device_id=device(place), device_id_type=MESH,
        )

    def sum_core(turn, k):
        for d in range(1, core):
            core_copy(turn, k, d).wait_recv()
        mine = parts[turn, k, :, :, c]
        for d in range(1, core):
            mine = mine + got_core[turn, k, d - 1]
        parts[turn, k, :, :, c] = mine
        for d in range(1, size[sum_axes(k)[0]]):
            sum_copy(turn, k, 0, d).start()
        return mine

    def sum_first(turn, k):
        first, second = sum_axes(k)
        got = got_near if first == "near" else got_far
        index = (turn, k, slice(None), b, c) if first == "near" else (turn, k, a, slice(None), c)
        mine = parts[index]
        for d in range(1, size[first]):
            sum_copy(turn, k, 0, d).wait_recv()
            mine = mine + got[turn, k, d - 1]
        parts[index] = mine
        for d in range(1, size[second]):
            sum_copy(turn, k, 1, d).start()

    def sum_second(turn, k):
        second = sum_axes(k)[1]
        got = got_near if second == "near" else got_far
        mine = parts[turn, k, a, b, c]
        for d in range(1, size[second]):
            sum_copy(turn, k, 1, d).wait_recv()
            mine = mine + got[turn, k, d - 1, 0]
        return mine

    def sum_end(turn):
        for k in range(chunks):
            for n in range(1, core):
                core_copy(turn, k, n).wait_send()
            for stage, axis in enumerate(sum_axes(k)):
                for n in range(1, size[axis]):
                    sum_copy(turn, k, stage, n).wait_send()

    def gather_rest(turn, beside):
        for k in range(chunks + 1):
            if k < chunks:
                gather_wait(turn, k, 0)
                gather_start(turn, k, 1)
                beside(k)
            if k > 0:
                gather_wait(turn, k - 1, 1)
                gather_start(turn, k - 1, 2)

    tiles_n = [(n, min(TILE, width - n)) for n in range(0, width, TILE)]

    def matmuls(turn, weigh):
        for k in range(chunks + 1):
            if k < chunks:
                gather_wait(turn, k, 2)
                pick_start(turn, k)
            if k > 0:
                pick_wait(turn, k - 1)
                high, low = split(chosen[...].reshape(op * ROWS, width))
                vector_h[k - 1] = high
                vector_l[k - 1] = low
        full = (op * rows, width)
        for start, wide in tiles_n:
            cols = pl.ds(start, wide)
            out = product3(
                vector_h[...].reshape(full), vector_l[...].reshape(full),
                right_h[:, cols], right_l[:, cols],
            ).reshape(chunks, op, ROWS, wide)
            for k in range(chunks):
                inner[:, pl.ds(k * ROWS, ROWS), :wide] = out[k]
            high, low = split(inner[:, :, :wide].reshape(op * rows, wide))
            inner_h[:, cols] = high
            inner_l[:, cols] = low
        for start, wide in tiles_n:
            cols = pl.ds(start, wide)
            parts[turn, :, :, :, :, :, cols] = product3(
                left_h[...].reshape(full), left_l[...].reshape(full),
                inner_h[:, cols], inner_l[:, cols],
            ).reshape(chunks, far, near, core, ROWS, wide)
        for k in range(chunks):
            for d in range(1, core):
                core_copy(turn, k, d).start()
        weighed = jnp.zeros((1, 1), F32)
        for k in range(chunks):
            weighed = weighed + total(weigh(k) * sum_core(turn, k))
        return weighed

    def finish(turn, red, ready, use):
        values = None
        for k in range(chunks + 2):
            if k < chunks:
                sum_first(turn, k)
            if k < 2:
                tile_advance(red, k)
            else:
                if k == 2:
                    values = ready()
                use(k - 2, values)

    for k in range(chunks):
        gather_start(0, k, 0)
    loads[0].wait()
    high, low = split(right_f[...])
    right_h[...] = high
    right_l[...] = low
    norm_part = total(raw[...] * raw[...])
    loads[1].wait()
    loads[3].wait()

    def split_left(k):
        high, low = split(left_f[:, pl.ds(k * ROWS, ROWS), :].reshape(op * ROWS, width))
        left_h[k] = high
        left_l[k] = low

    gather_rest(0, split_left)
    start_part = matmuls(0, lambda k: held[0][k][y])
    tile_start(0, (norm_part, start_part))

    def start_values():
        norm_raw = tile_read(0, 0)
        product_raw = tile_read(0, 1)
        return 1.0 / jnp.sqrt(norm_raw + EPS), product_raw / (norm_raw + EPS)

    kept = {"along": jnp.zeros((1, 1), F32)}

    def take_step(k, values):
        scale, rayleigh = values
        kept["scale"], kept["rayleigh"] = values
        here = pl.ds(k * ROWS, ROWS)
        v_zero = scale * raw[here, :]
        w_zero = scale * (sum_second(0, k) * mask[k * ROWS : (k + 1) * ROWS])
        update = (w_zero - rayleigh * v_zero) / den_v[here, :]
        applied[here, :] = w_zero
        step[here, :] = update
        held[1][k][y, a, b] = update
        gather_start(1, k, 0)
        kept["along"] = kept["along"] + total(v_zero * update)

    finish(0, 0, start_values, take_step)
    scale, rayleigh = kept["scale"], kept["rayleigh"]

    tile_start(1, (kept["along"],))

    def sum_along(k):
        if k in (1, 3):
            tile_advance(1, k // 2)

    gather_rest(1, sum_along)
    for stage in range(2):
        if 2 * stage + 1 >= chunks:
            tile_advance(1, stage)
    along = tile_read(1, 0)
    v_zero = scale * raw[...]
    update_perp = step[...] - along * v_zero
    step[...] = update_perp
    tail_part = total(update_perp * update_perp)
    couple_part = total(update_perp * applied[...])
    shift = along * scale
    corner_part = matmuls(1, lambda k: held[1][k][y] - shift * held[0][k][y])
    tile_start(2, (tail_part, couple_part, corner_part))

    def end_values():
        return end_scalars(tile_read, along, rayleigh)

    def give(k, values):
        gain, sine, cosine, lam = values
        here = pl.ds(k * ROWS, ROWS)
        w_zero = applied[here, :]
        w_one = gain * (sum_second(1, k) * mask[k * ROWS : (k + 1) * ROWS] - along * w_zero)
        new_vector = sine * (scale * raw[here, :]) - cosine * (gain * step[here, :])
        mixed = sine * w_zero - cosine * w_one
        new_ref[here, :] = new_vector
        corr_ref[here, :] = (mixed - lam * new_vector) / den_v[here, :]

    finish(1, 2, end_values, give)

    for turn in range(2):
        gather_end(turn)
        sum_end(turn)
    for red in range(3):
        for stage in range(2):
            for n in range(len(groups[stage])):
                tile_copy(red, stage, n).wait_send()


def fused(dims, sec, psi, left_env, right_env, denominators, source_sector, owner, orders):
    rows, _, width = psi.shape
    far, near, core = dims
    op = far * near * core
    chunks = rows // ROWS
    peers = far + near + core + sec - 4
    pairs = near * core * sec - 1 + far - 1
    vmem = pl.BlockSpec(memory_space=pltpu.VMEM)
    smem = pl.BlockSpec(memory_space=pltpu.SMEM)
    hbm = pl.BlockSpec(memory_space=pl.ANY)
    block = (ROWS, width)
    scratch = [pltpu.VMEM((sec, far, near) + block, F32)] * (2 * chunks) + [
        pltpu.VMEM((op, rows, width), F32),
        pltpu.VMEM((width, width), F32),
        pltpu.VMEM((chunks, op * ROWS, width), BF16),
        pltpu.VMEM((chunks, op * ROWS, width), BF16),
        pltpu.VMEM((width, width), BF16),
        pltpu.VMEM((width, width), BF16),
        pltpu.VMEM((op, rows, min(TILE, width)), F32),
        pltpu.VMEM((chunks, op * ROWS, width), BF16),
        pltpu.VMEM((chunks, op * ROWS, width), BF16),
        pltpu.VMEM((op * rows, width), BF16),
        pltpu.VMEM((op * rows, width), BF16),
        pltpu.VMEM((rows, width), F32),
        pltpu.VMEM((rows, width), F32),
        pltpu.VMEM((rows, width), F32),
        pltpu.VMEM((2, chunks, far, near, core) + block, F32),
        pltpu.VMEM((2, chunks, core - 1, far, near) + block, F32),
        pltpu.VMEM((2, chunks, near - 1, far) + block, F32),
        pltpu.VMEM((2, chunks, far - 1, near) + block, F32),
        pltpu.VMEM((2, chunks, core - 1, far, near) + block, F32),
        pltpu.VMEM((2, chunks, core - 1, far, near) + block, F32),
        pltpu.VMEM((far, near, core) + block, F32),
        pltpu.VMEM((rows, width), F32),
        pltpu.VMEM((rows, width), F32),
        pltpu.VMEM((3, 3, 8, 128), F32),
        pltpu.VMEM((3, pairs, 8, 128), F32),
        pltpu.SemaphoreType.DMA((4,)),
        pltpu.SemaphoreType.DMA((2, chunks, peers)),
        pltpu.SemaphoreType.DMA((2, chunks, peers)),
        pltpu.SemaphoreType.DMA((2, chunks, peers)),
        pltpu.SemaphoreType.DMA((2, chunks, peers)),
        pltpu.SemaphoreType.DMA((3, pairs)),
        pltpu.SemaphoreType.DMA((3, pairs)),
    ]
    flat = jax.ShapeDtypeStruct((rows, width), F32)
    new_vector, correction = pl.pallas_call(
        functools.partial(kernel, dims, sec),
        out_shape=(flat, flat),
        in_specs=[hbm, hbm, hbm, hbm, smem, smem, smem],
        out_specs=(vmem, vmem),
        scratch_shapes=scratch,
        compiler_params=pltpu.CompilerParams(
            collective_id=0, has_side_effects=True, vmem_limit_bytes=52 * 2**20
        ),
    )(
        psi,
        left_env.reshape(op, rows, width),
        right_env.reshape(width, width),
        denominators,
        source_sector,
        owner,
        orders,
    )
    return new_vector.reshape(psi.shape), correction.reshape(psi.shape)


def per_device(*arrays):
    psi, left_env = arrays[0], arrays[1]
    op = lax.axis_size("op")
    sec = lax.axis_size("sec")
    rows, sec_here, width = psi.shape
    core = 2 if op % 2 == 0 else 1
    chips = op // core
    near = max(n for n in range(1, chips + 1) if chips % n == 0 and n * n <= chips)
    dims = (chips // near, near, core)
    fits = rows % ROWS == 0 and width % 128 == 0 and left_env.shape[:2] == (1, 1)
    if fits and sec_here == 1 and min(dims) > 1 and sec > 1 and op * rows == width:
        return fused(dims, sec, *arrays)
    return general(*arrays)


def solution(mesh):
    placed = (
        P("op", "sec", None),
        P("op", "sec", None, None),
        P("op", "sec", None, None),
        P("op", "sec", None),
        P(),
        P(),
        P(),
    )
    return jax.shard_map(
        per_device,
        mesh=mesh,
        in_specs=placed,
        out_specs=(P("op", "sec", None), P("op", "sec", None)),
        check_vma=False,
    )
```

```python
import functools

import jax
import jax.numpy as jnp
from jax import lax
from jax.experimental import pallas as pl
from jax.experimental.pallas import tpu as pltpu
from jax.sharding import PartitionSpec as P

EPS = 1e-06
HIGH = lax.Precision.HIGHEST
MESH = pl.DeviceIdType.MESH
F32 = jnp.float32
BF16 = jnp.bfloat16
ROWS = 8
TILE = 256


def slot_sectors(owner):
    slots = jnp.arange(owner.shape[0], dtype=jnp.int32)
    hits = (owner[None, :] == slots[:, None]).astype(jnp.int32)
    return jnp.sum(hits * slots[None, :], axis=1)


def general(psi, left_env, right_env, denominators, source_sector, owner, orders):
    rows_here = psi.shape[0]
    sec_here = psi.shape[1]
    width = psi.shape[2]
    term_here = left_env.shape[0]
    op_size = lax.axis_size("op")
    sec_size = lax.axis_size("sec")
    op_pos = lax.axis_index("op")
    sec_pos = lax.axis_index("sec")
    sectors = slot_sectors(owner)
    sectors_here = lax.dynamic_slice_in_dim(sectors, sec_pos * sec_here, sec_here, 0)
    order_here = jnp.take(orders, sectors_here)
    row_ids = op_pos * rows_here + jnp.arange(rows_here, dtype=jnp.int32)
    col_ids = jnp.arange(width, dtype=jnp.int32)
    mask = (
        (row_ids[:, None, None] < order_here[None, :, None])
        & (col_ids[None, None, :] < order_here[None, :, None])
    ).astype(jnp.float32)
    source_all = jnp.take(owner, jnp.take(source_sector, sectors_here, axis=1))
    blocks = term_here * sec_here
    left_flat = left_env.reshape(blocks, width, width)
    right_flat = right_env.reshape(blocks, width, width)
    count = float(rows_here * sec_here * width * op_size * sec_size)

    def apply(vector):
        shard_all = lax.all_gather(vector, "sec", axis=1, tiled=True)
        outgoing = jnp.take(shard_all, source_all.reshape(-1), axis=1).reshape(
            rows_here, op_size, blocks, width
        )
        chosen = lax.all_to_all(outgoing, "op", split_axis=1, concat_axis=0, tiled=True).reshape(
            width, blocks, width
        )
        inner = jnp.einsum("apb,pbc->apc", chosen, right_flat, precision=HIGH)
        product = jnp.einsum("pxa,apc->xpc", left_flat, inner, precision=HIGH)
        whole = product.reshape(width, term_here, sec_here, width).sum(axis=1)
        summed = lax.psum_scatter(whole, "op", scatter_dimension=0, tiled=True)
        return summed * mask

    def partial_sum(first, second):
        return jnp.sum(first * second)

    v_raw = psi * mask
    w_raw = apply(v_raw)
    start_pair = lax.psum(
        jnp.stack([partial_sum(v_raw, v_raw), partial_sum(v_raw, w_raw)]), ("op", "sec")
    )
    norm_raw = start_pair[0] / count
    product_raw = start_pair[1] / count
    scale = 1.0 / jnp.sqrt(norm_raw + EPS)
    v_zero = scale * v_raw
    w_zero = scale * w_raw
    rayleigh = product_raw / (norm_raw + EPS)
    update = (w_zero - rayleigh * v_zero) / denominators
    along = lax.psum(partial_sum(v_zero, update), ("op", "sec")) / count
    update_perp = update - along * v_zero
    tail = lax.psum(partial_sum(update_perp, update_perp), ("op", "sec")) / count
    v_one = update_perp / jnp.sqrt(tail + EPS)
    w_one = apply(v_one)
    sub_pair = lax.psum(
        jnp.stack([partial_sum(v_one, w_one), partial_sum(v_one, w_zero)]), ("op", "sec")
    )
    corner = sub_pair[0] / count
    couple = sub_pair[1] / count
    angle = 0.5 * jnp.arctan2(2.0 * couple, rayleigh - corner)
    sine = jnp.sin(angle)
    cosine = jnp.cos(angle)
    new_vector = sine * v_zero - cosine * v_one
    applied = sine * w_zero - cosine * w_one
    lam = sine * sine * rayleigh + cosine * cosine * corner - 2.0 * sine * cosine * couple
    correction = (applied - lam * new_vector) / denominators
    return (new_vector, correction)


def split(value):
    high = value.astype(BF16)
    return high, (value - high.astype(F32)).astype(BF16)


def product3(ah, al, bh, bl):
    dot = functools.partial(jnp.dot, preferred_element_type=F32)
    return dot(ah, bh) + (dot(ah, bl) + dot(al, bh))


def end_scalars(tile_read, along, rayleigh):
    tail = tile_read(2, 0)
    perp_w_zero = tile_read(2, 1)
    perp_w = tile_read(2, 2) - along * perp_w_zero
    gain = 1.0 / jnp.sqrt(tail + EPS)
    corner = gain * gain * perp_w
    couple = gain * perp_w_zero
    down, across = 2.0 * couple, rayleigh - corner
    most = jnp.maximum(jnp.abs(down), jnp.abs(across))
    safe = jnp.where(most > 0.0, most, 1.0)
    down, across = down / safe, jnp.where(most > 0.0, across / safe, 1.0)
    length = jnp.sqrt(down * down + across * across)
    larger = jnp.sqrt(0.5 * (1.0 + jnp.abs(across) / length))
    smaller = 0.5 * jnp.abs(down) / (length * larger)
    sign = jnp.where(down < 0.0, -1.0, 1.0)
    cosine = jnp.where(across >= 0.0, larger, smaller)
    sine = sign * jnp.where(across >= 0.0, smaller, larger)
    lam = sine * sine * rayleigh + cosine * cosine * corner - 2.0 * sine * cosine * couple
    return gain, sine, cosine, lam


def row_chunks(rows):
    groups = rows // ROWS
    first = (groups + 1) // 2 * ROWS
    spans = [(0, first)] + ([(first, rows - first)] if rows > first else [])
    return len(spans), spans


def kernel(
    dims, sec, psi_hbm, left_hbm, right_hbm, den_hbm, source_ref, owner_ref, orders_ref,
    new_ref, corr_ref, *scratch
):
    far, near, core = dims
    chunks, spans = row_chunks(psi_hbm.shape[0])
    rows = psi_hbm.shape[0]
    width = psi_hbm.shape[2]
    op = far * near * core
    held = (scratch[:chunks], scratch[chunks : 2 * chunks])
    (left_f, right_f, left_h, left_l, right_h, right_l, vector_h, vector_l, inner_h, inner_l, raw,
     applied, step, parts, got_core, got_near, got_far, picked, got_picked, chosen, psi_v, den_v, tiles, got_tiles, load_sem,
     gather_send, gather_recv, sum_send, sum_recv, tile_send, tile_recv) = scratch[2 * chunks :]

    me = lax.axis_index("op")
    y = lax.axis_index("sec")
    c = lax.rem(me, core)
    b = lax.rem(lax.div(me, core), near)
    a = lax.div(me, core * near)
    where = {"far": a, "near": b, "core": c, "sec": y}
    size = {"far": far, "near": near, "core": core, "sec": sec}

    def at_rows(k):
        return pl.ds(spans[k][0], spans[k][1])

    def turned(axis, by):
        place = dict(where)
        place[axis] = lax.rem(where[axis] + by + size[axis], size[axis])
        return place

    def device(place):
        return ((place["far"] * near + place["near"]) * core + place["core"], place["sec"])

    every = [(axis, d) for axis in ("far", "near", "sec", "core") for d in range(1, size[axis])]
    around = [
        (("near", i), ("core", j), ("sec", l))
        for i in range(near) for j in range(core) for l in range(sec) if i + j + l > 0
    ]
    along_far = [(("far", d),) for d in range(1, far)]

    def moved(offset):
        place = dict(where)
        for axis, by in offset:
            place[axis] = lax.rem(where[axis] + by, size[axis])
        return place

    loads = [
        pltpu.make_async_copy(right_hbm, right_f, load_sem.at[0]),
        pltpu.make_async_copy(left_hbm, left_f, load_sem.at[1]),
        pltpu.make_async_copy(psi_hbm.at[:, 0], psi_v, load_sem.at[2]),
        pltpu.make_async_copy(den_hbm.at[:, 0], den_v, load_sem.at[3]),
    ]
    for n in (2, 0, 1, 3):
        loads[n].start()

    barrier = pltpu.get_barrier_semaphore()
    for offset in around + along_far:
        pl.semaphore_signal(
            barrier, inc=1, device_id=device(moved(offset)), device_id_type=MESH
        )

    sector = jnp.int32(0)
    for s in range(sec):
        sector = sector + jnp.where(owner_ref[s] == y, s, 0)
    order = orders_ref[sector]
    source = owner_ref[source_ref[me, sector]]

    row_ids = lax.broadcasted_iota(jnp.int32, (rows, width), 0) + me * rows
    col_ids = lax.broadcasted_iota(jnp.int32, (rows, width), 1)
    mask = ((row_ids < order) & (col_ids < order)).astype(F32)
    loads[2].wait()
    raw[...] = psi_v[...] * mask
    for k in range(chunks):
        held[0][k][y, a, b] = raw[at_rows(k), :]

    pl.semaphore_wait(barrier, len(around + along_far))

    def area(axes, place):
        pick = lambda axis: slice(None) if axis in axes else place[axis]
        return (pick("sec"), pick("far"), pick("near"))

    def sequence(k):
        return ("far", "near", "sec") if k % 2 == 0 else ("far", "sec", "near")

    slot_of = {pair: n for n, pair in enumerate(every)}

    def gather_copy(turn, k, stage, d, from_place, to_place):
        axes = sequence(k)
        block = held[turn][k].at[area(axes[:stage], from_place)]
        n = slot_of[(axes[stage], d)]
        return pltpu.make_async_remote_copy(
            src_ref=block, dst_ref=block,
            send_sem=gather_send.at[turn, k, n], recv_sem=gather_recv.at[turn, k, n],
            device_id=device(to_place), device_id_type=MESH,
        )

    def gather_start(turn, k, stage):
        axis = sequence(k)[stage]
        for d in range(1, size[axis]):
            gather_copy(turn, k, stage, d, where, turned(axis, d)).start()

    def gather_wait(turn, k, stage):
        axis = sequence(k)[stage]
        for d in range(1, size[axis]):
            gather_copy(turn, k, stage, d, turned(axis, -d), turned(axis, d)).wait_recv()

    def pick_copy(turn, k, d):
        n = slot_of[("core", d)]
        return pltpu.make_async_remote_copy(
            src_ref=picked.at[turn, d - 1, :, :, at_rows(k)],
            dst_ref=got_picked.at[turn, d - 1, :, :, at_rows(k)],
            send_sem=gather_send.at[turn, k, n], recv_sem=gather_recv.at[turn, k, n],
            device_id=device(turned("core", d)), device_id_type=MESH,
        )

    def pick_start(turn, k):
        for d in range(1, core):
            term = me - c + lax.rem(c + d, core)
            picked[turn, d - 1, :, :, at_rows(k)] = held[turn][k][owner_ref[source_ref[term, sector]]]
            pick_copy(turn, k, d).start()

    def pick_wait(turn, k):
        chosen[:, :, c, at_rows(k)] = held[turn][k][source]
        for d in range(1, core):
            pick_copy(turn, k, d).wait_recv()
            chosen[:, :, lax.rem(c + core - d, core), at_rows(k)] = got_picked[
                turn, d - 1, :, :, at_rows(k)
            ]

    def gather_end(turn):
        for k in range(chunks):
            for d in range(1, core):
                pick_copy(turn, k, d).wait_send()
            for stage, axis in enumerate(sequence(k)):
                for d in range(1, size[axis]):
                    gather_copy(turn, k, stage, d, where, turned(axis, d)).wait_send()

    groups = (around, along_far)

    def tile_copy(red, stage, n):
        slot = n + stage * len(around)
        return pltpu.make_async_remote_copy(
            src_ref=tiles.at[red, stage], dst_ref=got_tiles.at[red, slot],
            send_sem=tile_send.at[red, slot], recv_sem=tile_recv.at[red, slot],
            device_id=device(moved(groups[stage][n])), device_id_type=MESH,
        )

    def tile_send_all(red, stage):
        for n in range(len(groups[stage])):
            tile_copy(red, stage, n).start()

    def tile_start(red, values):
        line = lax.broadcasted_iota(jnp.int32, (8, 128), 0)
        tile = jnp.zeros((8, 128), F32)
        for n, value in enumerate(values):
            tile = jnp.where(line == n, value, tile)
        tiles[red, 0] = tile
        tile_send_all(red, 0)

    def tile_advance(red, stage):
        total = tiles[red, stage]
        for n in range(len(groups[stage])):
            tile_copy(red, stage, n).wait_recv()
            total = total + got_tiles[red, n + stage * len(around)]
        tiles[red, stage + 1] = total
        if stage == 0:
            tile_send_all(red, 1)

    count = float(rows * width * op * sec)

    def tile_read(red, n):
        return tiles[red, 2, pl.ds(n, 1), pl.ds(0, 1)] / count

    def total(value):
        return jnp.sum(value.reshape(-1, width), keepdims=True)

    def core_copy(turn, k, d):
        place = turned("core", d)
        return pltpu.make_async_remote_copy(
            src_ref=parts.at[turn, :, :, place["core"], at_rows(k)],
            dst_ref=got_core.at[turn, d - 1, :, :, at_rows(k)],
            send_sem=sum_send.at[turn, k, slot_of[("core", d)]],
            recv_sem=sum_recv.at[turn, k, slot_of[("core", d)]],
            device_id=device(place), device_id_type=MESH,
        )

    def sum_axes(k):
        return ("near", "far") if k % 2 == 0 else ("far", "near")

    def sum_copy(turn, k, stage, d):
        axis = sum_axes(k)[stage]
        place = turned(axis, d)
        if axis == "near":
            row = slice(None) if stage == 0 else a
            source_ref, target_ref = parts.at[turn, row, place["near"], c, at_rows(k)], got_near
        else:
            row = slice(None) if stage == 0 else b
            source_ref, target_ref = parts.at[turn, place["far"], row, c, at_rows(k)], got_far
        target = (turn, d - 1, slice(None) if stage == 0 else 0, at_rows(k))
        return pltpu.make_async_remote_copy(
            src_ref=source_ref, dst_ref=target_ref.at[target],
            send_sem=sum_send.at[turn, k, slot_of[(axis, d)]],
            recv_sem=sum_recv.at[turn, k, slot_of[(axis, d)]],
            device_id=device(place), device_id_type=MESH,
        )

    def sum_core(turn, k):
        for d in range(1, core):
            core_copy(turn, k, d).wait_recv()
        mine = parts[turn, :, :, c, at_rows(k)]
        for d in range(1, core):
            mine = mine + got_core[turn, d - 1, :, :, at_rows(k)]
        parts[turn, :, :, c, at_rows(k)] = mine
        for d in range(1, size[sum_axes(k)[0]]):
            sum_copy(turn, k, 0, d).start()
        return mine

    def sum_first(turn, k):
        first, second = sum_axes(k)
        got = got_near if first == "near" else got_far
        index = (turn,) + ((slice(None), b) if first == "near" else (a, slice(None))) + (c, at_rows(k))
        mine = parts[index]
        for d in range(1, size[first]):
            sum_copy(turn, k, 0, d).wait_recv()
            mine = mine + got[turn, d - 1, :, at_rows(k)]
        parts[index] = mine
        for d in range(1, size[second]):
            sum_copy(turn, k, 1, d).start()

    def sum_second(turn, k):
        second = sum_axes(k)[1]
        got = got_near if second == "near" else got_far
        mine = parts[turn, a, b, c, at_rows(k)]
        for d in range(1, size[second]):
            sum_copy(turn, k, 1, d).wait_recv()
            mine = mine + got[turn, d - 1, 0, at_rows(k)]
        return mine

    def sum_end(turn):
        for k in range(chunks):
            for n in range(1, core):
                core_copy(turn, k, n).wait_send()
            for stage, axis in enumerate(sum_axes(k)):
                for n in range(1, size[axis]):
                    sum_copy(turn, k, stage, n).wait_send()

    def gather_rest(turn, beside):
        for k in range(chunks + 1):
            if k < chunks:
                gather_wait(turn, k, 0)
                gather_start(turn, k, 1)
                beside(k)
            if k > 0:
                gather_wait(turn, k - 1, 1)
                gather_start(turn, k - 1, 2)

    tiles_n = [(n, min(TILE, width - n)) for n in range(0, width, TILE)]

    def matmuls(turn, weigh):
        for k in range(chunks + 1):
            if k < chunks:
                gather_wait(turn, k, 2)
                pick_start(turn, k)
            if k > 0:
                pick_wait(turn, k - 1)
        high, low = split(chosen[...].reshape(op * rows, width))
        vector_h[...] = high
        vector_l[...] = low
        for start, wide in tiles_n:
            cols = pl.ds(start, wide)
            high, low = split(
                product3(vector_h[...], vector_l[...], right_h[:, cols], right_l[:, cols])
            )
            inner_h[:, cols] = high
            inner_l[:, cols] = low
        for start, wide in tiles_n:
            cols = pl.ds(start, wide)
            parts[turn, :, :, :, :, cols] = product3(
                left_h[...], left_l[...], inner_h[:, cols], inner_l[:, cols]
            ).reshape(far, near, core, rows, wide)
        for k in range(chunks):
            for d in range(1, core):
                core_copy(turn, k, d).start()
        weighed = jnp.zeros((1, 1), F32)
        for k in range(chunks):
            weighed = weighed + total(weigh(k) * sum_core(turn, k))
        return weighed

    def finish(turn, red, ready, use):
        values = None
        for k in range(chunks + 2):
            if k < chunks:
                sum_first(turn, k)
            if k < 2:
                tile_advance(red, k)
            else:
                if k == 2:
                    values = ready()
                use(k - 2, values)

    for k in range(chunks):
        gather_start(0, k, 0)
    loads[0].wait()
    high, low = split(right_f[...])
    right_h[...] = high
    right_l[...] = low
    norm_part = total(raw[...] * raw[...])
    loads[1].wait()
    loads[3].wait()

    def split_left(k):
        if k == 0:
            high, low = split(left_f[...])
            left_h[...] = high
            left_l[...] = low

    gather_rest(0, split_left)
    start_part = matmuls(0, lambda k: held[0][k][y])
    tile_start(0, (norm_part, start_part))

    def start_values():
        norm_raw = tile_read(0, 0)
        product_raw = tile_read(0, 1)
        return 1.0 / jnp.sqrt(norm_raw + EPS), product_raw / (norm_raw + EPS)

    kept = {"along": jnp.zeros((1, 1), F32)}

    def take_step(k, values):
        scale, rayleigh = values
        kept["scale"], kept["rayleigh"] = values
        here = at_rows(k)
        v_zero = scale * raw[here, :]
        w_zero = scale * (sum_second(0, k) * mask[spans[k][0] : sum(spans[k])])
        update = (w_zero - rayleigh * v_zero) / den_v[here, :]
        applied[here, :] = w_zero
        step[here, :] = update
        held[1][k][y, a, b] = update
        gather_start(1, k, 0)
        kept["along"] = kept["along"] + total(v_zero * update)

    finish(0, 0, start_values, take_step)
    scale, rayleigh = kept["scale"], kept["rayleigh"]

    tile_start(1, (kept["along"],))

    def sum_along(k):
        if k in (1, 3):
            tile_advance(1, k // 2)

    gather_rest(1, sum_along)
    for stage in range(2):
        if 2 * stage + 1 >= chunks:
            tile_advance(1, stage)
    along = tile_read(1, 0)
    v_zero = scale * raw[...]
    update_perp = step[...] - along * v_zero
    step[...] = update_perp
    tail_part = total(update_perp * update_perp)
    couple_part = total(update_perp * applied[...])
    shift = along * scale
    corner_part = matmuls(1, lambda k: held[1][k][y] - shift * held[0][k][y])
    tile_start(2, (tail_part, couple_part, corner_part))

    def end_values():
        return end_scalars(tile_read, along, rayleigh)

    def give(k, values):
        gain, sine, cosine, lam = values
        here = at_rows(k)
        w_zero = applied[here, :]
        w_one = gain * (sum_second(1, k) * mask[spans[k][0] : sum(spans[k])] - along * w_zero)
        new_vector = sine * (scale * raw[here, :]) - cosine * (gain * step[here, :])
        mixed = sine * w_zero - cosine * w_one
        new_ref[here, :] = new_vector
        corr_ref[here, :] = (mixed - lam * new_vector) / den_v[here, :]

    finish(1, 2, end_values, give)

    for turn in range(2):
        gather_end(turn)
        sum_end(turn)
    for red in range(3):
        for stage in range(2):
            for n in range(len(groups[stage])):
                tile_copy(red, stage, n).wait_send()


def fused(dims, sec, psi, left_env, right_env, denominators, source_sector, owner, orders):
    rows, _, width = psi.shape
    far, near, core = dims
    op = far * near * core
    chunks, spans = row_chunks(rows)
    peers = far + near + core + sec - 4
    pairs = near * core * sec - 1 + far - 1
    vmem = pl.BlockSpec(memory_space=pltpu.VMEM)
    smem = pl.BlockSpec(memory_space=pltpu.SMEM)
    hbm = pl.BlockSpec(memory_space=pl.ANY)
    block = (rows, width)
    square = (width, width)
    scratch = [pltpu.VMEM((sec, far, near, size, width), F32) for _, size in spans] * 2
    scratch += [pltpu.VMEM(square, F32)] * 2 + [pltpu.VMEM(square, BF16)] * 8
    scratch += [pltpu.VMEM(block, F32)] * 3 + [
        pltpu.VMEM((2, far, near, core) + block, F32),
        pltpu.VMEM((2, core - 1, far, near) + block, F32),
        pltpu.VMEM((2, near - 1, far) + block, F32),
        pltpu.VMEM((2, far - 1, near) + block, F32),
        pltpu.VMEM((2, core - 1, far, near) + block, F32),
        pltpu.VMEM((2, core - 1, far, near) + block, F32),
        pltpu.VMEM((far, near, core) + block, F32),
        pltpu.VMEM(block, F32),
        pltpu.VMEM(block, F32),
        pltpu.VMEM((3, 3, 8, 128), F32),
        pltpu.VMEM((3, pairs, 8, 128), F32),
        pltpu.SemaphoreType.DMA((4,)),
        pltpu.SemaphoreType.DMA((2, chunks, peers)),
        pltpu.SemaphoreType.DMA((2, chunks, peers)),
        pltpu.SemaphoreType.DMA((2, chunks, peers)),
        pltpu.SemaphoreType.DMA((2, chunks, peers)),
        pltpu.SemaphoreType.DMA((3, pairs)),
        pltpu.SemaphoreType.DMA((3, pairs)),
    ]
    flat = jax.ShapeDtypeStruct((rows, width), F32)
    new_vector, correction = pl.pallas_call(
        functools.partial(kernel, dims, sec),
        out_shape=(flat, flat),
        in_specs=[hbm, hbm, hbm, hbm, smem, smem, smem],
        out_specs=(vmem, vmem),
        scratch_shapes=scratch,
        compiler_params=pltpu.CompilerParams(
            collective_id=0, has_side_effects=True, vmem_limit_bytes=52 * 2**20
        ),
    )(
        psi,
        left_env.reshape(width, width),
        right_env.reshape(width, width),
        denominators,
        source_sector,
        owner,
        orders,
    )
    return new_vector.reshape(psi.shape), correction.reshape(psi.shape)


def per_device(*arrays):
    psi, left_env = arrays[0], arrays[1]
    op = lax.axis_size("op")
    sec = lax.axis_size("sec")
    rows, sec_here, width = psi.shape
    core = 2 if op % 2 == 0 else 1
    chips = op // core
    near = max(n for n in range(1, chips + 1) if chips % n == 0 and n * n <= chips)
    dims = (chips // near, near, core)
    fits = rows % ROWS == 0 and width % 128 == 0 and left_env.shape[:2] == (1, 1)
    if fits and sec_here == 1 and min(dims) > 1 and sec > 1 and op * rows == width:
        return fused(dims, sec, *arrays)
    return general(*arrays)


def solution(mesh):
    placed = (
        P("op", "sec", None),
        P("op", "sec", None, None),
        P("op", "sec", None, None),
        P("op", "sec", None),
        P(),
        P(),
        P(),
    )
    return jax.shard_map(
        per_device,
        mesh=mesh,
        in_specs=placed,
        out_specs=(P("op", "sec", None), P("op", "sec", None)),
        check_vma=False,
    )
```
